128 devices in a mesh: gx: 16 (over z, y), gy: 8 (over x, core).
Axes of the slice: x: 4, y: 4, z: 4, core: 2. Of those that a mesh axis runs over, the one named last changes fastest.
Arguments:
- multipole: bfloat16 [16384, 3, 296], P(('gx', 'gy')), may hold values from -6 to 6
- m2m_ops: bfloat16 [8, 296, 296], replicated, may hold values from -0.125 to 0.125
- m2l_ops: bfloat16 [64, 296, 296], replicated, may hold values from -0.09375 to 0.09375
- leaf_targets: int32 [128, 64, 80], P(('gx', 'gy')), may hold values from -1 to 16383, as said below
- leaf_sources: int32 [128, 64, 80], P(('gx', 'gy')), may hold values from -1 to 16383, as said below
- parent_targets: int32 [128, 64, 32], P(('gx', 'gy')), may hold values from -1 to 2047, as said below
- parent_sources: int32 [128, 64, 32], P(('gx', 'gy')), may hold values from -1 to 2047, as said below
Outputs:
- leaf_local: float32 [16384, 3, 296], P(('gx', 'gy'))
- parent_local: float32 [2048, 3, 296], P(('gx', 'gy'))
The draws below stay inside these ranges and needn't reach their ends.
Inputs may be any that keep to these rules, and one draw needn't show every extreme that they name: Leaf box g belongs to device g // 128 of the combined axis gx+gy. An entry held at index d names target and source boxes of devices d - 2 to d + 2 (within the axis). A slot holds -1 in leaf_targets exactly when it holds -1 in leaf_sources. On every device some class has all 80 slots live. `leaf_sources`: same layout and reach as leaf_targets; -1 exactly in the same slots. `parent_targets`: parent box q belongs to device q // 16. An entry held at index d names target and source parents of devices d - 2 to d + 2. A slot holds -1 here exactly when it holds -1 in parent_sources. On every device some class has all 32 slots live. `parent_sources`: same layout and reach as parent_targets; -1 exactly in the same slots.
All inputs are finite; a program needn't handle non-finite values.
Results may differ from the reference program's by a relative error of at most 0.011.
Values may be sent and summed in bfloat16 or wider, within the bound.
A program may use at most 128 MiB of HBM per device.

```python
import jax
import jax.numpy as jnp
from jax import lax

P_SIZE = 296
CLASSES = 64
REACH = 2
BOX_DEV = 128
SLOT = 80
PSLOT = 32
PAR_DEV = 16
BOXES = 16384
PARENTS = 2048
N_GX = 16
N_GY = 8


def make_lists(key, slots, per_device):
    devices = N_GX * N_GY
    shape = (devices, CLASSES, slots)
    key_count = jax.random.fold_in(key, 11)
    key_target = jax.random.fold_in(key, 12)
    key_source = jax.random.fold_in(key, 13)
    device_row = jax.lax.broadcasted_iota(jnp.int32, shape, 0)
    class_col = jax.lax.broadcasted_iota(jnp.int32, (devices, CLASSES, 1), 1)
    slot_col = jax.lax.broadcasted_iota(jnp.int32, shape, 2)
    counts = jax.random.randint(key_count, (devices, CLASSES, 1), slots // 3, slots + 1)
    device_col = jax.lax.broadcasted_iota(jnp.int32, (devices, CLASSES, 1), 0)
    counts = jnp.where(class_col == device_col % CLASSES, slots, counts)
    live = slot_col < counts

    def pick(inner):
        offset = jax.random.randint(inner, shape, -REACH, REACH + 1)
        owner = jnp.clip(device_row + offset, 0, devices - 1)
        within = jax.random.randint(jax.random.fold_in(inner, 1), shape, 0, per_device)
        return jnp.where(live, owner * per_device + within, -1).astype(jnp.int32)
    return (pick(key_target), pick(key_source))


def draw_leaf_targets(key, part):
    return make_lists(key, SLOT, BOX_DEV)[0]


def draw_leaf_sources(key, part):
    return make_lists(key, SLOT, BOX_DEV)[1]


def draw_parent_targets(key, part):
    return make_lists(jax.random.fold_in(key, 7), PSLOT, BOX_DEV // 8)[0]


def draw_parent_sources(key, part):
    return make_lists(jax.random.fold_in(key, 7), PSLOT, BOX_DEV // 8)[1]


def block_scale(own_key, extent, shards, least, high):
    level, own = 1.0, jax.random.fold_in(own_key, 6)
    for position, shards_of in shards:
        draws = jnp.exp(jax.random.uniform(jax.random.fold_in(own, position), (shards_of,), jnp.float32, least / len(shards), high / len(shards)))
        level = level * jnp.repeat(draws, extent[position] // shards_of).reshape([-1 if axis == position else 1 for axis in range(len(extent))])
    return level


def noise(rng, dims, scale, bound, shards=(), held_as=jnp.bfloat16):
    factor_of = block_scale(rng, dims, shards, -0.22, 0.18) if shards else 1.0
    drawn = jax.random.normal(rng, dims, jnp.float32) * scale * factor_of
    return jnp.minimum(jnp.maximum(drawn, -bound), bound).astype(held_as)


def setup_inputs(seed: int = 0) -> dict:
    key_list = jax.random.split(jax.random.key(seed), 8)
    multipole = noise(key_list[0], (BOXES, 3, P_SIZE), 1.0, 6.0, ((0, 128),))
    m2m_ops = noise(key_list[1], (8, P_SIZE, P_SIZE), (8 * P_SIZE) ** -0.5, 0.125)
    m2l_ops = noise(key_list[2], (CLASSES, P_SIZE, P_SIZE), (16 * P_SIZE) ** -0.5, 0.09375)
    leaf_targets = draw_leaf_targets(jax.random.fold_in(key_list[7], 71), 0)
    leaf_sources = draw_leaf_sources(jax.random.fold_in(key_list[7], 71), 0)
    parent_targets = draw_parent_targets(jax.random.fold_in(key_list[7], 71), 0)
    parent_sources = draw_parent_sources(jax.random.fold_in(key_list[7], 71), 0)
    return {"multipole": multipole, "m2m_ops": m2m_ops, "m2l_ops": m2l_ops, "leaf_targets": leaf_targets, "leaf_sources": leaf_sources, "parent_targets": parent_targets, "parent_sources": parent_sources}


def translate(dense, targets, sources, ops, rows_dev):
    devices = targets.shape[0]
    span = 2 * REACH + 1
    width = ops.shape[2]
    ops_wide = ops.astype(jnp.float32)
    start_total = jnp.zeros(((devices + 2 * REACH) * rows_dev, 3, width), jnp.float32)

    def one_holder(holder, total):
        tgt = lax.dynamic_index_in_dim(targets, holder, 0, keepdims=False)
        src = lax.dynamic_index_in_dim(sources, holder, 0, keepdims=False)
        picked = dense[jnp.maximum(src, 0).astype(jnp.int32)].astype(jnp.float32)
        term = jnp.einsum("kscp,kpr->kscr", picked, ops_wide)
        base = (holder - REACH) * rows_dev
        where_to = jnp.where(tgt >= 0, tgt - base, span * rows_dev).astype(jnp.int32)
        window = jnp.zeros((span * rows_dev, 3, width), jnp.float32)
        window = window.at[where_to.reshape(-1)].add(term.reshape(-1, 3, width), mode="drop")
        window = lax.optimization_barrier(window.astype(jnp.bfloat16)).astype(jnp.float32)
        offset = (holder * rows_dev).astype(jnp.int32)
        current = lax.dynamic_slice_in_dim(total, offset, span * rows_dev, 0)
        return lax.dynamic_update_slice_in_dim(total, current + window, offset, 0)

    total = lax.fori_loop(jnp.int32(0), jnp.int32(devices), one_holder, start_total)
    return total[REACH * rows_dev:REACH * rows_dev + devices * rows_dev]


def reference(multipole, m2m_ops, m2l_ops, leaf_targets, leaf_sources, parent_targets, parent_sources):
    grouped = multipole.reshape(PARENTS, 8, 3, P_SIZE).astype(jnp.float32)
    parent_multipole = jnp.einsum("qocp,opr->qcr", grouped, m2m_ops.astype(jnp.float32)).astype(jnp.bfloat16)
    leaf_local = translate(multipole, leaf_targets, leaf_sources, m2l_ops, BOX_DEV)
    parent_local = translate(parent_multipole, parent_targets, parent_sources, m2l_ops, PAR_DEV)
    return leaf_local, parent_local
```

```python
import functools

import jax
import jax.numpy as jnp
from jax import lax
from jax.experimental import pallas as pl
from jax.experimental.pallas import tpu as pltpu
from jax.sharding import PartitionSpec as P

CLASSES = 64
SLOT = 80
PSLOT = 32
SLOTS = SLOT + PSLOT
P_SIZE = 296
BOX_DEV = 128
PAR_DEV = 16
SPAN = 5
LEAVES = SPAN * BOX_DEV
ROWS = LEAVES + SPAN * PAR_DEV
ACC_ROWS = ROWS + 8
CHAINS = 4
DEVICES = 128
N_GY = 8
MESH = pl.DeviceIdType.MESH
f32 = jnp.float32
bf16 = jnp.bfloat16
OFFSETS = (1, -1, 2, -2)


def dot_nt(a, b):
    return lax.dot_general(a, b, (((1,), (1,)), ((), ())), preferred_element_type=f32)


def here():
    return lax.axis_index("gx") * N_GY + lax.axis_index("gy")


def neighbour(offset):
    index = lax.rem(here() + (offset + DEVICES), DEVICES)
    return (lax.div(index, N_GY), lax.rem(index, N_GY))


def entry_barrier():
    barrier = pltpu.get_barrier_semaphore()
    for offset in OFFSETS:
        pl.semaphore_signal(barrier, inc=1, device_id=neighbour(offset), device_id_type=MESH)
    pl.semaphore_wait(barrier, len(OFFSETS))


def slot_of(offset):
    j = 2 - offset
    return j if j < 2 else j - 1


def exchange_kernel(
    mp, m2m, lt, ls, pt, ps, rem, par, idx, own, ops, par_own, send, recv, psend, precv, local
):
    get_own = pltpu.make_async_copy(mp, own, local.at[0])
    get_ops = pltpu.make_async_copy(m2m, ops, local.at[1])
    get_own.start()
    get_ops.start()
    entry_barrier()
    leaf_copies = []
    for n, offset in enumerate(OFFSETS):
        copy = pltpu.make_async_remote_copy(
            src_ref=mp,
            dst_ref=rem.at[slot_of(offset)],
            send_sem=send.at[n],
            recv_sem=recv.at[n],
            device_id=neighbour(offset),
            device_id_type=MESH,
        )
        copy.start()
        leaf_copies.append(copy)

    row = lax.broadcasted_iota(jnp.int32, (128, 128), 0)
    column = lax.broadcasted_iota(jnp.int32, (128, 128), 1)
    wanted = 8 * lax.rem(row, 16) + lax.div(row, 16)
    select = (column == wanted).astype(f32).astype(bf16)
    get_own.wait()
    by_octant = [dot_nt(select, own[c]).astype(bf16) for c in range(3)]
    get_ops.wait()
    total = jnp.zeros((48, P_SIZE), f32)
    for o in range(8):
        rows = jnp.concatenate([by_octant[c][16 * o : 16 * o + 16] for c in range(3)], axis=0)
        total = total + jnp.dot(rows, ops[o], preferred_element_type=f32)
    pieces = []
    for c in range(3):
        part = total[16 * c : 16 * c + 16]
        for q in range(2):
            par_own[2 * c + q] = part[:, 128 * q : 128 * q + 128].astype(bf16)
        pieces.append(
            jnp.concatenate([part[:, 256:296], jnp.zeros((16, 88), f32)], axis=1)
        )
    tails = pieces[0] + pltpu.roll(pieces[1], 40, 1) + pltpu.roll(pieces[2], 80, 1)
    par_own[6] = tails.astype(bf16)
    keep = pltpu.make_async_copy(par_own, par.at[2], local.at[2])
    keep.start()
    par_copies = []
    for n, offset in enumerate(OFFSETS):
        copy = pltpu.make_async_remote_copy(
            src_ref=par_own,
            dst_ref=par.at[2 - offset],
            send_sem=psend.at[n],
            recv_sem=precv.at[n],
            device_id=neighbour(offset),
            device_id_type=MESH,
        )
        copy.start()
        par_copies.append(copy)

    leaf_base = (here() - 2) * BOX_DEV
    par_base = (here() - 2) * PAR_DEV - LEAVES
    idx[...] = jnp.zeros_like(idx)
    idx[0, 0:64, 0:80] = jnp.where(ls[...] >= 0, ls[...] - leaf_base, 0)
    idx[1, 0:64, 0:80] = jnp.where(lt[...] >= 0, lt[...] - leaf_base, ROWS)
    idx[0, 64:96, 0:64] = jnp.where(ps[...] >= 0, ps[...] - par_base, 0)
    idx[1, 64:96, 0:64] = jnp.where(pt[...] >= 0, pt[...] - par_base, ROWS)

    keep.wait()
    for copy in leaf_copies + par_copies:
        copy.wait()


def translate_kernel(idx, mp, rem, par, ops_hbm, out, win, g, o0, o1, g1, ops, sem, *acc):
    gathered, terms = (g, g1), (o0, o1)

    def fetch(k):
        return pltpu.make_async_copy(ops_hbm.at[k], ops.at[k], sem.at[k])

    @pl.loop(0, CLASSES)
    def _(k):
        fetch(k).start()

    row = lax.broadcasted_iota(jnp.int32, (128, 128), 0)
    column = lax.broadcasted_iota(jnp.int32, (128, 128), 1)
    eye = (row == column).astype(f32).astype(bf16)
    for j in range(SPAN):
        src = mp if j == 2 else rem.at[j if j < 2 else j - 1]
        for c in range(3):
            m = dot_nt(eye, src[c, 0:256, :])
            for q in range(2):
                win[pl.ds(j * 1024 + 2 * c + q, 128, stride=8), :] = m[:, 128 * q : 128 * q + 128]
        tails = jnp.concatenate(
            [src[c, 256:296, :] for c in range(3)] + [jnp.zeros((8, 128), bf16)], axis=0
        )
        win[pl.ds(j * 1024 + 6, 128, stride=8), :] = dot_nt(eye, tails)
        for r in range(7):
            win[pl.ds((LEAVES + j * 16) * 8 + r, 16, stride=8), :] = par[j, r].astype(f32)
    zeros = jnp.zeros((64, 128), f32)
    for buffer in (o0, o1):

        @pl.loop(0, SLOTS // 8)
        def _(i):
            buffer[pl.ds(pl.multiple_of(i * 64, 64), 64), :] = zeros

    for a in acc:

        @pl.loop(0, ACC_ROWS // 8)
        def _(i):
            a[pl.ds(pl.multiple_of(i * 64, 64), 64), :] = zeros

    def at(which, k, s):
        place = idx[which, k, s] if s < SLOT else idx[which, 64 + s - SLOT, k]
        return pl.ds(pl.multiple_of(place * 8, 8), 8)

    def gather(k, b):
        for s in range(SLOTS):
            gathered[b][s * 8 : s * 8 + 8, :] = win[at(0, k, s), :]

    def scatter(k, b):
        for s in range(SLOTS):
            acc[s % CHAINS][at(1, k, s), :] += terms[b][s * 8 : s * 8 + 8, :]

    def multiply(k, b):
        rows = [gathered[b][pl.ds(r, SLOTS, stride=8), :] for r in range(7)]
        tails = (rows[6], pltpu.roll(rows[6], 88, 1), pltpu.roll(rows[6], 48, 1))
        x = jnp.concatenate(
            [
                jnp.concatenate(
                    [
                        rows[2 * c].astype(bf16),
                        rows[2 * c + 1].astype(bf16),
                        tails[c].astype(bf16)[:, :40],
                    ],
                    axis=1,
                )
                for c in range(3)
            ],
            axis=0,
        )
        y = jnp.dot(x, ops[k], preferred_element_type=f32)
        pieces = []
        for c in range(3):
            part = y[c * SLOTS : (c + 1) * SLOTS]
            for q in range(2):
                terms[b][pl.ds(2 * c + q, SLOTS, stride=8), :] = part[:, 128 * q : 128 * q + 128]
            pieces.append(
                jnp.concatenate([part[:, 256:296], jnp.zeros((SLOTS, 88), f32)], axis=1)
            )
        terms[b][pl.ds(6, SLOTS, stride=8), :] = (
            pieces[0] + pltpu.roll(pieces[1], 40, 1) + pltpu.roll(pieces[2], 80, 1)
        )

    gather(0, 0)

    @pl.loop(0, CLASSES // 2)
    def _(i):
        k = 2 * i
        fetch(k).wait()
        fetch(k + 1).wait()
        gather(k + 1, 1)
        multiply(k, 0)
        scatter(jnp.maximum(k - 1, 0), 1)
        gather(jnp.minimum(k + 2, CLASSES - 1), 0)
        multiply(k + 1, 1)
        scatter(k, 0)

    scatter(CLASSES - 1, 1)

    def total(start, count):
        rows = pl.ds(start, count, stride=8)
        return functools.reduce(lambda p, q: p + q, [a[rows, :] for a in acc])

    for j in range(SPAN):
        for r in range(7):
            leaf = total(j * 1024 + r, 128).astype(bf16)
            out[j, r, 0:128, :] = dot_nt(eye, leaf).astype(bf16)
            out[j, r, 128:144, :] = total(LEAVES * 8 + j * 128 + r, 16).astype(bf16)


def sum_kernel(partial, leaf, parent, own, got, send, recv, local):
    get_own = pltpu.make_async_copy(partial.at[2], own, local)
    get_own.start()
    entry_barrier()
    copies = []
    for n, offset in enumerate(OFFSETS):
        copy = pltpu.make_async_remote_copy(
            src_ref=partial.at[2 + offset],
            dst_ref=got.at[n],
            send_sem=send.at[n],
            recv_sem=recv.at[n],
            device_id=neighbour(offset),
            device_id_type=MESH,
        )
        copy.start()
        copies.append(copy)
    get_own.wait()
    for copy in copies:
        copy.wait()

    def total(r):
        s = own[r].astype(f32)
        for n in range(4):
            s = s + got[n, r].astype(f32)
        return s

    for c in range(3):
        for q in range(2):
            s = total(2 * c + q)
            leaf[c, 128 * q : 128 * q + 128, :] = s[0:128]
            parent[c, :, 128 * q : 128 * q + 128] = s[128:144]
    s = total(6)
    for c in range(3):
        leaf[c, 256:296, :] = s[40 * c : 40 * c + 40]
        shifted = s[128:144] if c == 0 else pltpu.roll(s[128:144], 128 - 40 * c, 1)
        parent[c, :, 256:296] = shifted[:, :40]


def on_device(multipole, m2m_ops, m2l_ops, lt, ls, pt, ps):
    mp = jnp.transpose(multipole, (1, 2, 0))
    pt, ps = jnp.transpose(pt[0]), jnp.transpose(ps[0])
    vmem = pl.BlockSpec(memory_space=pltpu.VMEM)
    smem = pl.BlockSpec(memory_space=pltpu.SMEM)
    anywhere = pl.BlockSpec(memory_space=pl.ANY)
    rem, par, idx = pl.pallas_call(
        exchange_kernel,
        out_shape=(
            jax.ShapeDtypeStruct((4, 3, P_SIZE, BOX_DEV), bf16),
            jax.ShapeDtypeStruct((SPAN, 7, PAR_DEV, 128), bf16),
            jax.ShapeDtypeStruct((2, 104, 128), jnp.int32),
        ),
        in_specs=[anywhere, anywhere, vmem, vmem, vmem, vmem],
        out_specs=(anywhere, anywhere, vmem),
        scratch_shapes=[
            pltpu.VMEM((3, P_SIZE, BOX_DEV), bf16),
            pltpu.VMEM((8, P_SIZE, P_SIZE), bf16),
            pltpu.VMEM((7, PAR_DEV, 128), bf16),
            pltpu.SemaphoreType.DMA((4,)),
            pltpu.SemaphoreType.DMA((4,)),
            pltpu.SemaphoreType.DMA((4,)),
            pltpu.SemaphoreType.DMA((4,)),
            pltpu.SemaphoreType.DMA((3,)),
        ],
        compiler_params=pltpu.CompilerParams(
            collective_id=0, has_side_effects=True, vmem_limit_bytes=32 * 1024 * 1024
        ),
        name="exchange",
    )(mp, m2m_ops, lt[0], ls[0], pt, ps)
    partial = pl.pallas_call(
        translate_kernel,
        out_shape=jax.ShapeDtypeStruct((SPAN, 7, BOX_DEV + PAR_DEV, 128), bf16),
        in_specs=[smem, vmem, vmem, vmem, anywhere],
        out_specs=vmem,
        scratch_shapes=[pltpu.VMEM((ACC_ROWS * 8, 128), f32)]
        + [pltpu.VMEM((SLOTS * 8, 128), f32)] * 4
        + [pltpu.VMEM((CLASSES, P_SIZE, P_SIZE), bf16), pltpu.SemaphoreType.DMA((CLASSES,))]
        + [pltpu.VMEM((ACC_ROWS * 8, 128), f32)] * CHAINS,
        compiler_params=pltpu.CompilerParams(vmem_limit_bytes=56 * 1024 * 1024),
        name="translate",
    )(idx, mp, rem, par, m2l_ops)
    leaf, parent = pl.pallas_call(
        sum_kernel,
        out_shape=(
            jax.ShapeDtypeStruct((3, P_SIZE, BOX_DEV), f32),
            jax.ShapeDtypeStruct((3, PAR_DEV, P_SIZE), f32),
        ),
        in_specs=[anywhere],
        out_specs=(vmem, vmem),
        scratch_shapes=[
            pltpu.VMEM((7, BOX_DEV + PAR_DEV, 128), bf16),
            pltpu.VMEM((4, 7, BOX_DEV + PAR_DEV, 128), bf16),
            pltpu.SemaphoreType.DMA((4,)),
            pltpu.SemaphoreType.DMA((4,)),
            pltpu.SemaphoreType.DMA,
        ],
        compiler_params=pltpu.CompilerParams(
            collective_id=1, has_side_effects=True, vmem_limit_bytes=32 * 1024 * 1024
        ),
        name="sums",
    )(partial)
    return jnp.transpose(leaf, (2, 0, 1)), jnp.transpose(parent, (1, 0, 2))


def solution(mesh):
    boxes = P(("gx", "gy"), None, None)
    return jax.shard_map(
        on_device,
        mesh=mesh,
        in_specs=(boxes, P(), P(), boxes, boxes, boxes, boxes),
        out_specs=(boxes, boxes),
        check_vma=False,
    )
```

```python
import functools

import jax
import jax.numpy as jnp
from jax import lax
from jax.experimental import pallas as pl
from jax.experimental.pallas import tpu as pltpu
from jax.sharding import PartitionSpec as P

CLASSES = 64
SLOT = 80
PSLOT = 32
BUCKETS = (3, 4, 5, 6, 7)
SLOTS = SLOT + PSLOT
P_SIZE = 296
BOX_DEV = 128
PAR_DEV = 16
SPAN = 5
LEAVES = SPAN * BOX_DEV
ROWS = LEAVES + SPAN * PAR_DEV
ACC_ROWS = ROWS + 8
CHAINS = 4
DEVICES = 128
VMEM_BYTES = 63 * 1024 * 1024
N_GY = 8
MESH = pl.DeviceIdType.MESH
f32 = jnp.float32
bf16 = jnp.bfloat16
OFFSETS = (1, -1, 2, -2)


def dot_nt(a, b):
    return lax.dot_general(a, b, (((1,), (1,)), ((), ())), preferred_element_type=f32)


def mask16(x):
    return x.astype(f32).astype(bf16)


def iota(shape, dim):
    return lax.broadcasted_iota(jnp.int32, shape, dim)


def here():
    return lax.axis_index("gx") * N_GY + lax.axis_index("gy")


def neighbour(offset):
    index = lax.rem(here() + (offset + DEVICES), DEVICES)
    return (lax.div(index, N_GY), lax.rem(index, N_GY))


def entry_barrier():
    barrier = pltpu.get_barrier_semaphore()
    for offset in OFFSETS:
        pl.semaphore_signal(barrier, inc=1, device_id=neighbour(offset), device_id_type=MESH)
    pl.semaphore_wait(barrier, len(OFFSETS))


def slot_of(offset):
    j = 2 - offset
    return j if j < 2 else j - 1


def prepare_lists(ls, lt, ps, pt, leaf_base, par_base, values, place, packed, idx):
    eye = mask16(iota((64, 64), 0) == iota((64, 64), 1))

    def together(leaf, parent):
        low = jnp.concatenate(
            [jnp.zeros((80, 64), bf16), mask16(parent), jnp.zeros((16, 64), bf16)], axis=0
        )
        high = jnp.concatenate([leaf.astype(f32), jnp.zeros((64, 48), f32)], axis=1)
        return high + dot_nt(eye, low)

    leaf_live, par_live = ls[...] >= 0, ps[...] >= 0
    sl = jnp.where(leaf_live, ls[...] - leaf_base, 0)
    tl = jnp.where(leaf_live, lt[...] - leaf_base, 0)
    sp = jnp.where(par_live, ps[...] - par_base, 0)
    tp = jnp.where(par_live, pt[...] - par_base, 0)
    parts = [
        together(sl >> 3, sp >> 3),
        together(sl & 7, sp & 7),
        together(tl >> 3, tp >> 3),
        together(tl & 7, tp & 7),
        together(leaf_live, par_live),
    ]
    live = parts[4].astype(bf16)
    earlier = mask16(iota((128, 128), 0) < iota((128, 128), 1))
    before = jnp.dot(live, earlier, preferred_element_type=f32)
    place[...] = jnp.where(parts[4] > 0.5, before, 200.0)
    values[...] = jnp.zeros_like(values)
    for q, part in enumerate(parts):
        values[pl.ds(q, 64, stride=8), :] = part
    wanted = iota((128, 128), 0).astype(f32)

    @pl.loop(0, CLASSES, unroll=16)
    def _(k):
        hit = mask16(wanted == place[pl.ds(k, 1), :])
        rows = pl.ds(pl.multiple_of(k * 8, 8), 8)
        packed[rows, :] = dot_nt(values[rows, :].astype(bf16), hit)

    ones = jnp.ones((128, 128), bf16)
    count = jnp.dot(live, ones, preferred_element_type=f32)
    count_row = dot_nt(ones[0:16], live)[0:1, :]
    row, column = iota((64, 64), 0), iota((64, 64), 1)
    count_column = count[:, 0:64]
    ahead = mask16(
        (count_row < count_column) | ((count_row == count_column) & (column < row))
    )
    rank = dot_nt(ones[0:16, 0:64], ahead)[0:1, :]
    perm = mask16(rank == row.astype(f32))

    def sort(v):
        return jnp.dot(perm, v.astype(bf16), preferred_element_type=f32)

    s_high, s_low, t_high, t_low, used = (
        sort(packed[pl.ds(q, 64, stride=8), :]) for q in range(5)
    )
    order = sort(iota((64, 128), 0).astype(f32))
    lane = iota((64, 128), 1)
    source = (s_high * 8 + s_low) * 8
    target = jnp.where(used > 0.5, t_high * 8 + t_low, float(ROWS)) * 8
    idx[0, 0:64, :] = jnp.where(lane == 120, order, source).astype(jnp.int32)
    idx[1, 0:64, :] = target.astype(jnp.int32)
    fits = mask16(count <= (16 * lane).astype(f32))
    pairs = jnp.dot(ones[0:16, 0:64], fits, preferred_element_type=f32)[0:8]
    idx[0, 64:72, :] = pairs.astype(jnp.int32) >> 1
    idx[1, 64:72, :] = jnp.zeros((8, 128), jnp.int32)


def exchange_kernel(
    mp, m2m, lt_in, ls_in, pt_in, ps_in, rem, par, idx_out,
    own, ops, par_own, lt, ls, pt, ps, values, place, packed, idx,
    send, recv, psend, precv, local,
):
    staged = [
        pltpu.make_async_copy(src, dst, local.at[n])
        for n, (src, dst) in enumerate(
            ((mp, own), (m2m, ops), (lt_in, lt), (ls_in, ls), (pt_in, pt), (ps_in, ps))
        )
    ]
    for copy in staged:
        copy.start()
    entry_barrier()
    leaf_copies = []
    for n, offset in enumerate(OFFSETS):
        copy = pltpu.make_async_remote_copy(
            src_ref=mp,
            dst_ref=rem.at[slot_of(offset)],
            send_sem=send.at[n],
            recv_sem=recv.at[n],
            device_id=neighbour(offset),
            device_id_type=MESH,
        )
        copy.start()
        leaf_copies.append(copy)
    for copy in staged:
        copy.wait()

    row = iota((128, 128), 0)
    select = mask16(iota((128, 128), 1) == 8 * (row & 15) + (row >> 4))
    by_octant = [dot_nt(select, own[c]).astype(bf16) for c in range(3)]
    total = jnp.zeros((48, P_SIZE), f32)
    for o in range(8):
        rows = jnp.concatenate([by_octant[c][16 * o : 16 * o + 16] for c in range(3)], axis=0)
        total = total + jnp.dot(rows, ops[o], preferred_element_type=f32)
    pieces = []
    for c in range(3):
        part = total[16 * c : 16 * c + 16]
        for q in range(2):
            par_own[2 * c + q] = part[:, 128 * q : 128 * q + 128].astype(bf16)
        pieces.append(jnp.concatenate([part[:, 256:296], jnp.zeros((16, 88), f32)], axis=1))
    tails = pieces[0] + pltpu.roll(pieces[1], 40, 1) + pltpu.roll(pieces[2], 80, 1)
    par_own[6] = tails.astype(bf16)
    keep = pltpu.make_async_copy(par_own, par.at[2], local.at[6])
    keep.start()
    par_copies = []
    for n, offset in enumerate(OFFSETS):
        copy = pltpu.make_async_remote_copy(
            src_ref=par_own,
            dst_ref=par.at[2 - offset],
            send_sem=psend.at[n],
            recv_sem=precv.at[n],
            device_id=neighbour(offset),
            device_id_type=MESH,
        )
        copy.start()
        par_copies.append(copy)

    leaf_base = (here() - 2) * BOX_DEV
    par_base = (here() - 2) * PAR_DEV - LEAVES
    prepare_lists(ls, lt, ps, pt, leaf_base, par_base, values, place, packed, idx)
    put = pltpu.make_async_copy(idx, idx_out, local.at[7])
    put.start()

    keep.wait()
    put.wait()
    for copy in leaf_copies + par_copies:
        copy.wait()


def translate_kernel(
    idx_in, mp, rem, par_in, ops_in, out,
    idx, blocks, par, result, win, g0, g1, o0, o1, ops, ops_sem, sem, *acc,
):
    gathered, terms = (g0, g1), (o0, o1)
    get_idx = pltpu.make_async_copy(idx_in, idx, sem.at[0])
    get_idx.start()
    get_blocks = []
    for j in range(SPAN):
        src = mp if j == 2 else rem.at[j if j < 2 else j - 1]
        get_blocks.append(pltpu.make_async_copy(src, blocks.at[j], sem.at[1 + j]))
        get_blocks[j].start()
    get_par = pltpu.make_async_copy(par_in, par, sem.at[6])
    get_par.start()

    zeros = jnp.zeros((448, 128), f32)
    for a in acc:

        @pl.loop(0, ACC_ROWS * 8 // 448)
        def _(i):
            a[pl.ds(pl.multiple_of(i * 448, 448), 448), :] = zeros

    for buffer in terms:
        buffer[...] = jnp.zeros_like(buffer)

    get_idx.wait()

    def fetch(r):
        return pltpu.make_async_copy(ops_in.at[idx[0, r, 120]], ops.at[r], ops_sem.at[r])

    @pl.loop(0, CLASSES)
    def _(r):
        fetch(r).start()

    eye = mask16(iota((128, 128), 0) == iota((128, 128), 1))
    get_par.wait()
    for j in range(SPAN):
        get_blocks[j].wait()
        for c in range(3):
            m = dot_nt(eye, blocks[j, c, 0:256, :])
            for q in range(2):
                win[pl.ds(j * 1024 + 2 * c + q, 128, stride=8), :] = m[:, 128 * q : 128 * q + 128]
        tails = jnp.concatenate(
            [blocks[j, c, 256:296, :] for c in range(3)] + [jnp.zeros((8, 128), bf16)], axis=0
        )
        win[pl.ds(j * 1024 + 6, 128, stride=8), :] = dot_nt(eye, tails)
        for r in range(7):
            win[pl.ds((LEAVES + j * 16) * 8 + r, 16, stride=8), :] = par[j, r].astype(f32)

    def at(which, k, s):
        return pl.ds(pl.multiple_of(idx[which, k, s], 8), 8)

    def gather(k, b, n):
        for s in range(n):
            gathered[b][s * 8 : s * 8 + 8, :] = win[at(0, k, s), :]

    def scatter(k, b, n):
        for s in range(n):
            acc[s % CHAINS][at(1, k, s), :] += terms[b][s * 8 : s * 8 + 8, :]

    def multiply(k, b, n):
        rows = [gathered[b][pl.ds(r, n, stride=8), :] for r in range(7)]
        tails = (rows[6], pltpu.roll(rows[6], 88, 1), pltpu.roll(rows[6], 48, 1))
        x = jnp.concatenate(
            [
                jnp.concatenate(
                    [
                        rows[2 * c].astype(bf16),
                        rows[2 * c + 1].astype(bf16),
                        tails[c].astype(bf16)[:, :40],
                    ],
                    axis=1,
                )
                for c in range(3)
            ],
            axis=0,
        )
        y = jnp.dot(x, ops[k], preferred_element_type=f32)
        pieces = []
        for c in range(3):
            part = y[c * n : (c + 1) * n]
            for q in range(2):
                terms[b][pl.ds(2 * c + q, n, stride=8), :] = part[:, 128 * q : 128 * q + 128]
            pieces.append(jnp.concatenate([part[:, 256:296], jnp.zeros((n, 88), f32)], axis=1))
        terms[b][pl.ds(6, n, stride=8), :] = (
            pieces[0] + pltpu.roll(pieces[1], 40, 1) + pltpu.roll(pieces[2], 80, 1)
        )

    start = 0
    for bucket in BUCKETS:
        n = 16 * bucket
        end = idx[0, 64, bucket]

        @pl.when(end > start)
        def _():
            gather(2 * start, 0, n)

        @pl.loop(start, end)
        def _(i):
            k = 2 * i
            fetch(k).wait()
            fetch(k + 1).wait()
            gather(k + 1, 1, n)
            multiply(k, 0, n)
            scatter(jnp.maximum(k - 1, 0), 1, n)
            gather(jnp.minimum(k + 2, CLASSES - 1), 0, n)
            multiply(k + 1, 1, n)
            scatter(k, 0, n)

        start = end
    scatter(CLASSES - 1, 1, SLOTS)

    def total(first, count):
        rows = pl.ds(first, count, stride=8)
        return functools.reduce(lambda p, q: p + q, [a[rows, :] for a in acc])

    puts = []
    for j in range(SPAN):
        for r in range(7):
            leaf = total(j * 1024 + r, 128).astype(bf16)
            result[j, r, 0:128, :] = dot_nt(eye, leaf).astype(bf16)
            result[j, r, 128:144, :] = total(LEAVES * 8 + j * 128 + r, 16).astype(bf16)
        puts.append(pltpu.make_async_copy(result.at[j], out.at[j], sem.at[7 + j]))
        puts[j].start()
    for put in puts:
        put.wait()


def sum_kernel(partial, leaf, parent, own, got, send, recv, local):
    get_own = pltpu.make_async_copy(partial.at[2], own, local)
    get_own.start()
    entry_barrier()
    copies = []
    for n, offset in enumerate(OFFSETS):
        copy = pltpu.make_async_remote_copy(
            src_ref=partial.at[2 + offset],
            dst_ref=got.at[n],
            send_sem=send.at[n],
            recv_sem=recv.at[n],
            device_id=neighbour(offset),
            device_id_type=MESH,
        )
        copy.start()
        copies.append(copy)
    get_own.wait()
    for copy in copies:
        copy.wait()

    def total(r):
        s = own[r].astype(f32)
        for n in range(4):
            s = s + got[n, r].astype(f32)
        return s

    for c in range(3):
        for q in range(2):
            s = total(2 * c + q)
            leaf[c, 128 * q : 128 * q + 128, :] = s[0:128]
            parent[c, :, 128 * q : 128 * q + 128] = s[128:144]
    s = total(6)
    for c in range(3):
        leaf[c, 256:296, :] = s[40 * c : 40 * c + 40]
        shifted = s[128:144] if c == 0 else pltpu.roll(s[128:144], 128 - 40 * c, 1)
        parent[c, :, 256:296] = shifted[:, :40]


def on_device(multipole, m2m_ops, m2l_ops, lt, ls, pt, ps):
    mp = jnp.transpose(multipole, (1, 2, 0))
    pt, ps = jnp.transpose(pt[0]), jnp.transpose(ps[0])
    vmem = pl.BlockSpec(memory_space=pltpu.VMEM)
    hbm = pl.BlockSpec(memory_space=pltpu.HBM)
    semaphores = pltpu.SemaphoreType.DMA
    rem, par, idx = pl.pallas_call(
        exchange_kernel,
        out_shape=(
            jax.ShapeDtypeStruct((4, 3, P_SIZE, BOX_DEV), bf16),
            jax.ShapeDtypeStruct((SPAN, 7, PAR_DEV, 128), bf16),
            jax.ShapeDtypeStruct((2, 72, 128), jnp.int32),
        ),
        in_specs=[hbm] * 6,
        out_specs=(hbm, hbm, hbm),
        scratch_shapes=[
            pltpu.VMEM((3, P_SIZE, BOX_DEV), bf16),
            pltpu.VMEM((8, P_SIZE, P_SIZE), bf16),
            pltpu.VMEM((7, PAR_DEV, 128), bf16),
            pltpu.VMEM((CLASSES, SLOT), jnp.int32),
            pltpu.VMEM((CLASSES, SLOT), jnp.int32),
            pltpu.VMEM((PSLOT, CLASSES), jnp.int32),
            pltpu.VMEM((PSLOT, CLASSES), jnp.int32),
            pltpu.VMEM((CLASSES * 8, 128), f32),
            pltpu.VMEM((CLASSES, 128), f32),
            pltpu.VMEM((CLASSES * 8, 128), f32),
            pltpu.VMEM((2, 72, 128), jnp.int32),
            semaphores((4,)),
            semaphores((4,)),
            semaphores((4,)),
            semaphores((4,)),
            semaphores((8,)),
        ],
        compiler_params=pltpu.CompilerParams(
            collective_id=0, has_side_effects=True, vmem_limit_bytes=VMEM_BYTES
        ),
        name="exchange",
    )(mp, m2m_ops, lt[0], ls[0], pt, ps)
    partial = pl.pallas_call(
        translate_kernel,
        out_shape=jax.ShapeDtypeStruct((SPAN, 7, BOX_DEV + PAR_DEV, 128), bf16),
        in_specs=[hbm] * 5,
        out_specs=hbm,
        scratch_shapes=[
            pltpu.SMEM((2, 72, 128), jnp.int32),
            pltpu.VMEM((SPAN, 3, P_SIZE, BOX_DEV), bf16),
            pltpu.VMEM((SPAN, 7, PAR_DEV, 128), bf16),
            pltpu.VMEM((SPAN, 7, BOX_DEV + PAR_DEV, 128), bf16),
            pltpu.VMEM((ROWS * 8, 128), f32),
        ]
        + [pltpu.VMEM((SLOTS * 8, 128), f32)] * 4
        + [pltpu.VMEM((CLASSES, P_SIZE, P_SIZE), bf16), semaphores((CLASSES,)), semaphores((12,))]
        + [pltpu.VMEM((ACC_ROWS * 8, 128), f32)] * CHAINS,
        compiler_params=pltpu.CompilerParams(vmem_limit_bytes=VMEM_BYTES),
        name="translate",
    )(idx, mp, rem, par, m2l_ops)
    leaf, parent = pl.pallas_call(
        sum_kernel,
        out_shape=(
            jax.ShapeDtypeStruct((3, P_SIZE, BOX_DEV), f32),
            jax.ShapeDtypeStruct((3, PAR_DEV, P_SIZE), f32),
        ),
        in_specs=[hbm],
        out_specs=(vmem, vmem),
        scratch_shapes=[
            pltpu.VMEM((7, BOX_DEV + PAR_DEV, 128), bf16),
            pltpu.VMEM((4, 7, BOX_DEV + PAR_DEV, 128), bf16),
            semaphores((4,)),
            semaphores((4,)),
            semaphores,
        ],
        compiler_params=pltpu.CompilerParams(
            collective_id=1, has_side_effects=True, vmem_limit_bytes=VMEM_BYTES
        ),
        name="sums",
    )(partial)
    return jnp.transpose(leaf, (2, 0, 1)), jnp.transpose(parent, (1, 0, 2))


def solution(mesh):
    boxes = P(("gx", "gy"), None, None)
    return jax.shard_map(
        on_device,
        mesh=mesh,
        in_specs=(boxes, P(), P(), boxes, boxes, boxes, boxes),
        out_specs=(boxes, boxes),
        check_vma=False,
    )
```

```python
import functools

import jax
import jax.numpy as jnp
from jax import lax
from jax.experimental import pallas as pl
from jax.experimental.pallas import tpu as pltpu
from jax.sharding import PartitionSpec as P

CLASSES = 64
SLOT = 80
PSLOT = 32
BUCKETS = (3, 4, 5, 6, 7)
SLOTS = SLOT + PSLOT
P_SIZE = 296
BOX_DEV = 128
PAR_DEV = 16
SPAN = 5
LEAVES = SPAN * BOX_DEV
ROWS = LEAVES + SPAN * PAR_DEV
ACC_ROWS = ROWS + 8
CHAINS = 4
DEVICES = 128
VMEM_BYTES = 63 * 1024 * 1024
N_GY = 8
MESH = pl.DeviceIdType.MESH
f32 = jnp.float32
bf16 = jnp.bfloat16


def dot_nt(a, b):
    return lax.dot_general(a, b, (((1,), (1,)), ((), ())), preferred_element_type=f32)


def mask16(x):
    return x.astype(f32).astype(bf16)


def iota(shape, dim):
    return lax.broadcasted_iota(jnp.int32, shape, dim)


def here():
    return lax.axis_index("gx") * N_GY + lax.axis_index("gy")


def device_at(offset):
    index = lax.rem(here() + (offset + DEVICES), DEVICES)
    return (lax.div(index, N_GY), lax.rem(index, N_GY))


def sides():
    me = here()
    out = 2 * lax.rem(me, 2) - 1
    ahead, behind = me + 2 * out, me - 2 * out
    return out, (ahead >= 0) & (ahead < DEVICES), (behind >= 0) & (behind < DEVICES)


def entry_barrier():
    barrier = pltpu.get_barrier_semaphore()
    out, out_ok, in_ok = sides()

    def greet(offset):
        pl.semaphore_signal(barrier, inc=1, device_id=device_at(offset), device_id_type=MESH)

    greet(-out)

    @pl.when(out_ok)
    def _():
        greet(out)
        greet(2 * out)

    @pl.when(in_ok)
    def _():
        greet(-2 * out)

    pl.semaphore_wait(barrier, 1 + 2 * out_ok.astype(jnp.int32) + in_ok.astype(jnp.int32))


def remote(src, dst, send, recv, n, offset):
    return pltpu.make_async_remote_copy(
        src_ref=src,
        dst_ref=dst,
        send_sem=send.at[n],
        recv_sem=recv.at[n],
        device_id=device_at(offset),
        device_id_type=MESH,
    )


class Spread:
    def __init__(self, own, blocks, cut, send, recv):
        out, self.out_ok, self.in_ok = sides()
        first, rest = pl.ds(0, cut), pl.ds(cut, own.shape[0] - cut)
        copy = functools.partial(remote, send=send, recv=recv)
        self.sibling = copy(own, blocks.at[2 + out], n=0, offset=-out)
        self.behind = copy(own, blocks.at[2 + 2 * out], n=1, offset=-2 * out)
        self.near = copy(own.at[first], blocks.at[2 - out, first], n=2, offset=out)
        self.far = copy(own.at[rest], blocks.at[2 - 2 * out, rest], n=3, offset=2 * out)
        self.relay_near = copy(
            blocks.at[2 + out, first], blocks.at[2 + 2 * out, first], n=4, offset=-out
        )
        self.relay_far = copy(
            blocks.at[2 - 2 * out, rest], blocks.at[2 - out, rest], n=5, offset=-out
        )

    def start(self):
        @pl.when(self.out_ok)
        def _():
            self.near.start()
            self.far.start()

        @pl.when(self.in_ok)
        def _():
            self.behind.start()

        self.sibling.start()

    def relay(self):
        @pl.when(self.out_ok)
        def _():
            self.near.wait_recv()
            self.relay_near.start()

        @pl.when(self.in_ok)
        def _():
            self.far.wait_recv()
            self.relay_far.start()

    def finish(self):
        self.sibling.wait()

        @pl.when(self.out_ok)
        def _():
            self.near.wait_send()
            self.far.wait_send()
            self.behind.wait_recv()
            self.relay_near.wait_send()
            self.relay_far.wait_recv()

        @pl.when(self.in_ok)
        def _():
            self.behind.wait_send()
            self.relay_far.wait_send()
            self.relay_near.wait_recv()


def prepare_lists(ls, lt, ps, pt, leaf_base, par_base, values, place, packed, idx):
    eye = mask16(iota((64, 64), 0) == iota((64, 64), 1))

    def together(leaf, parent):
        low = jnp.concatenate(
            [jnp.zeros((80, 64), bf16), mask16(parent), jnp.zeros((16, 64), bf16)], axis=0
        )
        high = jnp.concatenate([leaf.astype(f32), jnp.zeros((64, 48), f32)], axis=1)
        return high + dot_nt(eye, low)

    leaf_live, par_live = ls[...] >= 0, ps[...] >= 0
    sl = jnp.where(leaf_live, ls[...] - leaf_base, 0)
    tl = jnp.where(leaf_live, lt[...] - leaf_base, 0)
    sp = jnp.where(par_live, ps[...] - par_base, 0)
    tp = jnp.where(par_live, pt[...] - par_base, 0)
    parts = [
        together(sl >> 3, sp >> 3),
        together(sl & 7, sp & 7),
        together(tl >> 3, tp >> 3),
        together(tl & 7, tp & 7),
        together(leaf_live, par_live),
    ]
    live = parts[4].astype(bf16)
    earlier = mask16(iota((128, 128), 0) < iota((128, 128), 1))
    before = jnp.dot(live, earlier, preferred_element_type=f32)
    place[...] = jnp.where(parts[4] > 0.5, before, 200.0)
    values[...] = jnp.zeros_like(values)
    for q, part in enumerate(parts):
        values[pl.ds(q, 64, stride=8), :] = part
    wanted = iota((128, 128), 0).astype(f32)

    @pl.loop(0, CLASSES, unroll=16)
    def _(k):
        hit = mask16(wanted == place[pl.ds(k, 1), :])
        rows = pl.ds(pl.multiple_of(k * 8, 8), 8)
        packed[rows, :] = dot_nt(values[rows, :].astype(bf16), hit)

    ones = jnp.ones((128, 128), bf16)
    count = jnp.dot(live, ones, preferred_element_type=f32)
    count_row = dot_nt(ones[0:16], live)[0:1, :]
    row, column = iota((64, 64), 0), iota((64, 64), 1)
    count_column = count[:, 0:64]
    ahead = mask16(
        (count_row < count_column) | ((count_row == count_column) & (column < row))
    )
    rank = dot_nt(ones[0:16, 0:64], ahead)[0:1, :]
    perm = mask16(rank == row.astype(f32))

    def sort(v):
        return jnp.dot(perm, v.astype(bf16), preferred_element_type=f32)

    s_high, s_low, t_high, t_low, used = (
        sort(packed[pl.ds(q, 64, stride=8), :]) for q in range(5)
    )
    order = sort(iota((64, 128), 0).astype(f32))
    lane = iota((64, 128), 1)
    source = (s_high * 8 + s_low) * 8
    target = jnp.where(used > 0.5, t_high * 8 + t_low, float(ROWS)) * 8
    idx[0, 0:64, :] = jnp.where(lane == 120, order, source).astype(jnp.int32)
    idx[1, 0:64, :] = target.astype(jnp.int32)
    fits = mask16(count <= (16 * lane).astype(f32))
    pairs = jnp.dot(ones[0:16, 0:64], fits, preferred_element_type=f32)[0:8]
    idx[0, 64:72, :] = pairs.astype(jnp.int32) >> 1
    idx[1, 64:72, :] = jnp.zeros((8, 128), jnp.int32)


def exchange_kernel(
    mp, m2m, lt_in, ls_in, pt_in, ps_in, rem, par, idx_out,
    own, ops, par_own, lt, ls, pt, ps, values, place, packed, idx,
    send, recv, psend, precv, local,
):
    staged = [
        pltpu.make_async_copy(src, dst, local.at[n])
        for n, (src, dst) in enumerate(
            ((mp, own), (m2m, ops), (lt_in, lt), (ls_in, ls), (pt_in, pt), (ps_in, ps))
        )
    ]
    for copy in staged:
        copy.start()
    entry_barrier()
    leaves = Spread(mp, rem, 2, send, recv)
    leaves.start()
    for copy in staged:
        copy.wait()

    row = iota((128, 128), 0)
    select = mask16(iota((128, 128), 1) == 8 * (row & 15) + (row >> 4))
    by_octant = [dot_nt(select, own[c]).astype(bf16) for c in range(3)]
    total = jnp.zeros((48, P_SIZE), f32)
    for o in range(8):
        rows = jnp.concatenate([by_octant[c][16 * o : 16 * o + 16] for c in range(3)], axis=0)
        total = total + jnp.dot(rows, ops[o], preferred_element_type=f32)
    pieces = []
    for c in range(3):
        part = total[16 * c : 16 * c + 16]
        for q in range(2):
            par_own[2 * c + q] = part[:, 128 * q : 128 * q + 128].astype(bf16)
        pieces.append(jnp.concatenate([part[:, 256:296], jnp.zeros((16, 88), f32)], axis=1))
    tails = pieces[0] + pltpu.roll(pieces[1], 40, 1) + pltpu.roll(pieces[2], 80, 1)
    par_own[6] = tails.astype(bf16)
    keep = pltpu.make_async_copy(par_own, par.at[2], local.at[6])
    keep.start()
    parents = Spread(par_own, par, 4, psend, precv)
    parents.start()

    leaf_base = (here() - 2) * BOX_DEV
    par_base = (here() - 2) * PAR_DEV - LEAVES
    prepare_lists(ls, lt, ps, pt, leaf_base, par_base, values, place, packed, idx)
    put = pltpu.make_async_copy(idx, idx_out, local.at[7])
    put.start()

    leaves.relay()
    parents.relay()
    keep.wait()
    put.wait()
    leaves.finish()
    parents.finish()


def translate_kernel(
    idx_in, mp, rem, par_in, ops_in, out,
    idx, blocks, par, result, win, g0, g1, o0, o1, ops, ops_sem, sem, *acc,
):
    gathered, terms = (g0, g1), (o0, o1)
    get_idx = pltpu.make_async_copy(idx_in, idx, sem.at[0])
    get_idx.start()
    get_blocks = []
    for j in range(SPAN):
        src = mp if j == 2 else rem.at[j]
        get_blocks.append(pltpu.make_async_copy(src, blocks.at[j], sem.at[1 + j]))
        get_blocks[j].start()
    get_par = pltpu.make_async_copy(par_in, par, sem.at[6])
    get_par.start()

    zeros = jnp.zeros((448, 128), f32)
    for a in acc:

        @pl.loop(0, ACC_ROWS * 8 // 448)
        def _(i):
            a[pl.ds(pl.multiple_of(i * 448, 448), 448), :] = zeros

    for buffer in terms:
        buffer[...] = jnp.zeros_like(buffer)

    get_idx.wait()

    def fetch(r):
        return pltpu.make_async_copy(ops_in.at[idx[0, r, 120]], ops.at[r], ops_sem.at[r])

    @pl.loop(0, CLASSES)
    def _(r):
        fetch(r).start()

    eye = mask16(iota((128, 128), 0) == iota((128, 128), 1))
    get_par.wait()
    for j in range(SPAN):
        get_blocks[j].wait()
        for c in range(3):
            m = dot_nt(eye, blocks[j, c, 0:256, :])
            for q in range(2):
                win[pl.ds(j * 1024 + 2 * c + q, 128, stride=8), :] = m[:, 128 * q : 128 * q + 128]
        tails = jnp.concatenate(
            [blocks[j, c, 256:296, :] for c in range(3)] + [jnp.zeros((8, 128), bf16)], axis=0
        )
        win[pl.ds(j * 1024 + 6, 128, stride=8), :] = dot_nt(eye, tails)
        for r in range(7):
            win[pl.ds((LEAVES + j * 16) * 8 + r, 16, stride=8), :] = par[j, r].astype(f32)

    def at(which, k, s):
        return pl.ds(pl.multiple_of(idx[which, k, s], 8), 8)

    def gather(k, b, n):
        for s in range(n):
            gathered[b][s * 8 : s * 8 + 8, :] = win[at(0, k, s), :]

    def scatter(k, b, n):
        for s in range(n):
            acc[s % CHAINS][at(1, k, s), :] += terms[b][s * 8 : s * 8 + 8, :]

    def multiply(k, b, n):
        rows = [gathered[b][pl.ds(r, n, stride=8), :] for r in range(7)]
        tails = (rows[6], pltpu.roll(rows[6], 88, 1), pltpu.roll(rows[6], 48, 1))
        x = jnp.concatenate(
            [
                jnp.concatenate(
                    [
                        rows[2 * c].astype(bf16),
                        rows[2 * c + 1].astype(bf16),
                        tails[c].astype(bf16)[:, :40],
                    ],
                    axis=1,
                )
                for c in range(3)
            ],
            axis=0,
        )
        y = jnp.dot(x, ops[k], preferred_element_type=f32)
        pieces = []
        for c in range(3):
            part = y[c * n : (c + 1) * n]
            for q in range(2):
                terms[b][pl.ds(2 * c + q, n, stride=8), :] = part[:, 128 * q : 128 * q + 128]
            pieces.append(jnp.concatenate([part[:, 256:296], jnp.zeros((n, 88), f32)], axis=1))
        terms[b][pl.ds(6, n, stride=8), :] = (
            pieces[0] + pltpu.roll(pieces[1], 40, 1) + pltpu.roll(pieces[2], 80, 1)
        )

    start = 0
    for bucket in BUCKETS:
        n = 16 * bucket
        end = idx[0, 64, bucket]

        @pl.when(end > start)
        def _():
            gather(2 * start, 0, n)

        @pl.loop(start, end)
        def _(i):
            k = 2 * i
            fetch(k).wait()
            fetch(k + 1).wait()
            gather(k + 1, 1, n)
            multiply(k, 0, n)
            scatter(jnp.maximum(k - 1, 0), 1, n)
            gather(jnp.minimum(k + 2, CLASSES - 1), 0, n)
            multiply(k + 1, 1, n)
            scatter(k, 0, n)

        start = end
    scatter(CLASSES - 1, 1, SLOTS)

    def total(first, count):
        rows = pl.ds(first, count, stride=8)
        return functools.reduce(lambda p, q: p + q, [a[rows, :] for a in acc])

    puts = []
    for j in range(SPAN):
        for r in range(7):
            leaf = total(j * 1024 + r, 128).astype(bf16)
            result[j, r, 0:128, :] = dot_nt(eye, leaf).astype(bf16)
            result[j, r, 128:144, :] = total(LEAVES * 8 + j * 128 + r, 16).astype(bf16)
        puts.append(pltpu.make_async_copy(result.at[j], out.at[j], sem.at[7 + j]))
        puts[j].start()
    for put in puts:
        put.wait()


def sum_kernel(
    partial, leaf, parent, own, mine_near, mine_far, from_near, from_far, side, behind, ahead,
    send, recv, local,
):
    out, out_ok, in_ok = sides()
    first, rest = pl.ds(0, 4), pl.ds(4, 3)
    staged = [
        pltpu.make_async_copy(src, dst, local.at[n])
        for n, (src, dst) in enumerate(
            (
                (partial.at[2], own),
                (partial.at[2 + out, first], mine_near),
                (partial.at[2 - 2 * out, rest], mine_far),
            )
        )
    ]
    for copy in staged:
        copy.start()
    copy = functools.partial(remote, send=send, recv=recv)
    lend_far = copy(partial.at[2 - 2 * out, first], from_near, n=0, offset=-out)
    lend_near = copy(partial.at[2 + out, rest], from_far, n=1, offset=-out)
    to_side = copy(partial.at[2 - out], side, n=2, offset=-out)
    to_far = copy(partial.at[2 + 2 * out], behind, n=3, offset=2 * out)
    sum_near = copy(mine_near, ahead.at[first], n=4, offset=out)
    sum_far = copy(mine_far, ahead.at[rest], n=5, offset=-2 * out)
    entry_barrier()

    @pl.when(in_ok)
    def _():
        lend_far.start()

    @pl.when(out_ok)
    def _():
        lend_near.start()
        to_far.start()

    to_side.start()
    for c in staged:
        c.wait()

    def add(mine, theirs):
        mine[...] = (mine[...].astype(f32) + theirs[...].astype(f32)).astype(bf16)

    @pl.when(out_ok)
    def _():
        lend_far.wait_recv()
        add(mine_near, from_near)
        sum_near.start()

    @pl.when(in_ok)
    def _():
        lend_near.wait_recv()
        add(mine_far, from_far)
        sum_far.start()

    to_side.wait()

    @pl.when(out_ok)
    def _():
        lend_near.wait_send()
        to_far.wait_send()
        sum_near.wait()
        sum_far.wait_recv()

    @pl.when(in_ok)
    def _():
        lend_far.wait_send()
        to_far.wait_recv()
        sum_far.wait_send()

    @pl.when(jnp.logical_not(out_ok))
    def _():
        ahead[...] = jnp.zeros_like(ahead)

    @pl.when(jnp.logical_not(in_ok))
    def _():
        behind[...] = jnp.zeros_like(behind)

    def total(r):
        s = own[r].astype(f32) + side[r].astype(f32)
        return s + behind[r].astype(f32) + ahead[r].astype(f32)

    for c in range(3):
        for q in range(2):
            s = total(2 * c + q)
            leaf[c, 128 * q : 128 * q + 128, :] = s[0:128]
            parent[c, :, 128 * q : 128 * q + 128] = s[128:144]
    s = total(6)
    for c in range(3):
        leaf[c, 256:296, :] = s[40 * c : 40 * c + 40]
        shifted = s[128:144] if c == 0 else pltpu.roll(s[128:144], 128 - 40 * c, 1)
        parent[c, :, 256:296] = shifted[:, :40]


def write_kernel(leaf_in, parent_in, leaf, parent, sem):
    copies = [
        pltpu.make_async_copy(src.at[c], dst.at[c], sem.at[2 * c + n])
        for c in range(3)
        for n, (src, dst) in enumerate(((leaf_in, leaf), (parent_in, parent)))
    ]
    for copy in copies:
        copy.start()
    for copy in copies:
        copy.wait()


def on_device(multipole, m2m_ops, m2l_ops, lt, ls, pt, ps):
    mp = jnp.transpose(multipole, (1, 2, 0))
    pt, ps = jnp.transpose(pt[0]), jnp.transpose(ps[0])
    vmem = pl.BlockSpec(memory_space=pltpu.VMEM)
    hbm = pl.BlockSpec(memory_space=pltpu.HBM)
    semaphores = pltpu.SemaphoreType.DMA
    rem, par, idx = pl.pallas_call(
        exchange_kernel,
        out_shape=(
            jax.ShapeDtypeStruct((SPAN, 3, P_SIZE, BOX_DEV), bf16),
            jax.ShapeDtypeStruct((SPAN, 7, PAR_DEV, 128), bf16),
            jax.ShapeDtypeStruct((2, 72, 128), jnp.int32),
        ),
        in_specs=[hbm] * 6,
        out_specs=(hbm, hbm, hbm),
        scratch_shapes=[
            pltpu.VMEM((3, P_SIZE, BOX_DEV), bf16),
            pltpu.VMEM((8, P_SIZE, P_SIZE), bf16),
            pltpu.VMEM((7, PAR_DEV, 128), bf16),
            pltpu.VMEM((CLASSES, SLOT), jnp.int32),
            pltpu.VMEM((CLASSES, SLOT), jnp.int32),
            pltpu.VMEM((PSLOT, CLASSES), jnp.int32),
            pltpu.VMEM((PSLOT, CLASSES), jnp.int32),
            pltpu.VMEM((CLASSES * 8, 128), f32),
            pltpu.VMEM((CLASSES, 128), f32),
            pltpu.VMEM((CLASSES * 8, 128), f32),
            pltpu.VMEM((2, 72, 128), jnp.int32),
            semaphores((6,)),
            semaphores((6,)),
            semaphores((6,)),
            semaphores((6,)),
            semaphores((8,)),
        ],
        compiler_params=pltpu.CompilerParams(
            collective_id=0, has_side_effects=True, vmem_limit_bytes=VMEM_BYTES
        ),
        name="exchange",
    )(mp, m2m_ops, lt[0], ls[0], pt, ps)
    partial = pl.pallas_call(
        translate_kernel,
        out_shape=jax.ShapeDtypeStruct((SPAN, 7, BOX_DEV + PAR_DEV, 128), bf16),
        in_specs=[hbm] * 5,
        out_specs=hbm,
        scratch_shapes=[
            pltpu.SMEM((2, 72, 128), jnp.int32),
            pltpu.VMEM((SPAN, 3, P_SIZE, BOX_DEV), bf16),
            pltpu.VMEM((SPAN, 7, PAR_DEV, 128), bf16),
            pltpu.VMEM((SPAN, 7, BOX_DEV + PAR_DEV, 128), bf16),
            pltpu.VMEM((ROWS * 8, 128), f32),
        ]
        + [pltpu.VMEM((SLOTS * 8, 128), f32)] * 4
        + [pltpu.VMEM((CLASSES, P_SIZE, P_SIZE), bf16), semaphores((CLASSES,)), semaphores((12,))]
        + [pltpu.VMEM((ACC_ROWS * 8, 128), f32)] * CHAINS,
        compiler_params=pltpu.CompilerParams(vmem_limit_bytes=VMEM_BYTES),
        name="translate",
    )(idx, mp, rem, par, m2l_ops)
    block = (7, BOX_DEV + PAR_DEV, 128)
    results = (
        jax.ShapeDtypeStruct((3, P_SIZE, BOX_DEV), f32),
        jax.ShapeDtypeStruct((3, PAR_DEV, P_SIZE), f32),
    )
    leaf, parent = pl.pallas_call(
        sum_kernel,
        out_shape=results,
        in_specs=[hbm],
        out_specs=(vmem, vmem),
        scratch_shapes=[
            pltpu.VMEM(block, bf16),
            pltpu.VMEM((4,) + block[1:], bf16),
            pltpu.VMEM((3,) + block[1:], bf16),
            pltpu.VMEM((4,) + block[1:], bf16),
            pltpu.VMEM((3,) + block[1:], bf16),
            pltpu.VMEM(block, bf16),
            pltpu.VMEM(block, bf16),
            pltpu.VMEM(block, bf16),
            semaphores((6,)),
            semaphores((6,)),
            semaphores((3,)),
        ],
        compiler_params=pltpu.CompilerParams(
            collective_id=1, has_side_effects=True, vmem_limit_bytes=VMEM_BYTES
        ),
        name="sums",
    )(partial)
    leaf, parent = pl.pallas_call(
        write_kernel,
        out_shape=results,
        in_specs=[hbm, hbm],
        out_specs=(hbm, hbm),
        scratch_shapes=[semaphores((6,))],
        compiler_params=pltpu.CompilerParams(vmem_limit_bytes=VMEM_BYTES),
        name="write",
    )(leaf, parent)
    return jnp.transpose(leaf, (2, 0, 1)), jnp.transpose(parent, (1, 0, 2))


def solution(mesh):
    boxes = P(("gx", "gy"), None, None)
    return jax.shard_map(
        on_device,
        mesh=mesh,
        in_specs=(boxes, P(), P(), boxes, boxes, boxes, boxes),
        out_specs=(boxes, boxes),
        check_vma=False,
    )
```

```python
import functools

import jax
import jax.numpy as jnp
from jax import lax
from jax.experimental import pallas as pl
from jax.experimental.pallas import tpu as pltpu
from jax.sharding import PartitionSpec as P

CLASSES = 64
SLOT = 80
PSLOT = 32
BUCKETS = (3, 4, 5, 6, 7)
SLOTS = SLOT + PSLOT
P_SIZE = 296
BOX_DEV = 128
PAR_DEV = 16
SPAN = 5
LEAVES = SPAN * BOX_DEV
ROWS = LEAVES + SPAN * PAR_DEV
ACC_ROWS = ROWS + 8
CHAINS = 4
DEVICES = 128
VMEM_BYTES = 63 * 1024 * 1024
N_GY = 8
MESH = pl.DeviceIdType.MESH
f32 = jnp.float32
bf16 = jnp.bfloat16


def dot_nt(a, b):
    return lax.dot_general(a, b, (((1,), (1,)), ((), ())), preferred_element_type=f32)


def mask16(x):
    return x.astype(f32).astype(bf16)


def iota(shape, dim):
    return lax.broadcasted_iota(jnp.int32, shape, dim)


def here():
    return lax.axis_index("gx") * N_GY + lax.axis_index("gy")


def device_at(offset):
    index = lax.rem(here() + (offset + DEVICES), DEVICES)
    return (lax.div(index, N_GY), lax.rem(index, N_GY))


def sides():
    me = here()
    out = 2 * lax.rem(me, 2) - 1
    ahead, behind = me + 2 * out, me - 2 * out
    return out, (ahead >= 0) & (ahead < DEVICES), (behind >= 0) & (behind < DEVICES)


def entry_barrier():
    barrier = pltpu.get_barrier_semaphore()
    out, out_ok, in_ok = sides()

    def greet(offset):
        pl.semaphore_signal(barrier, inc=1, device_id=device_at(offset), device_id_type=MESH)

    greet(-out)

    @pl.when(out_ok)
    def _():
        greet(out)
        greet(2 * out)

    @pl.when(in_ok)
    def _():
        greet(-2 * out)

    pl.semaphore_wait(barrier, 1 + 2 * out_ok.astype(jnp.int32) + in_ok.astype(jnp.int32))


def remote(src, dst, send, recv, n, offset):
    return pltpu.make_async_remote_copy(
        src_ref=src,
        dst_ref=dst,
        send_sem=send.at[n],
        recv_sem=recv.at[n],
        device_id=device_at(offset),
        device_id_type=MESH,
    )


class Spread:
    def __init__(self, own, blocks, cut, send, recv):
        out, self.out_ok, self.in_ok = sides()
        first, rest = pl.ds(0, cut), pl.ds(cut, own.shape[0] - cut)
        copy = functools.partial(remote, send=send, recv=recv)
        self.sibling = copy(own, blocks.at[2 + out], n=0, offset=-out)
        self.behind = copy(own, blocks.at[2 + 2 * out], n=1, offset=-2 * out)
        self.near = copy(own.at[first], blocks.at[2 - out, first], n=2, offset=out)
        self.far = copy(own.at[rest], blocks.at[2 - 2 * out, rest], n=3, offset=2 * out)
        self.relay_near = copy(
            blocks.at[2 + out, first], blocks.at[2 + 2 * out, first], n=4, offset=-out
        )
        self.relay_far = copy(
            blocks.at[2 - 2 * out, rest], blocks.at[2 - out, rest], n=5, offset=-out
        )

    def start(self):
        @pl.when(self.out_ok)
        def _():
            self.near.start()
            self.far.start()

        self.sibling.start()

    def start_unshared(self):
        @pl.when(self.in_ok)
        def _():
            self.behind.start()

    def relay(self):
        @pl.when(self.out_ok)
        def _():
            self.near.wait_recv()
            self.relay_near.start()

        @pl.when(self.in_ok)
        def _():
            self.far.wait_recv()
            self.relay_far.start()

    def finish(self):
        self.sibling.wait()

        @pl.when(self.out_ok)
        def _():
            self.near.wait_send()
            self.far.wait_send()
            self.behind.wait_recv()
            self.relay_near.wait_send()
            self.relay_far.wait_recv()

        @pl.when(self.in_ok)
        def _():
            self.behind.wait_send()
            self.relay_far.wait_send()
            self.relay_near.wait_recv()


def prepare_lists(ls, lt, ps, pt, leaf_base, par_base, values, place, packed, idx):
    eye = mask16(iota((64, 64), 0) == iota((64, 64), 1))

    def together(leaf, parent):
        low = jnp.concatenate(
            [jnp.zeros((80, 64), bf16), mask16(parent), jnp.zeros((16, 64), bf16)], axis=0
        )
        high = jnp.concatenate([leaf.astype(f32), jnp.zeros((64, 48), f32)], axis=1)
        return high + dot_nt(eye, low)

    leaf_live, par_live = ls[...] >= 0, ps[...] >= 0
    sl = jnp.where(leaf_live, ls[...] - leaf_base, 0)
    tl = jnp.where(leaf_live, lt[...] - leaf_base, 0)
    sp = jnp.where(par_live, ps[...] - par_base, 0)
    tp = jnp.where(par_live, pt[...] - par_base, 0)
    parts = [
        together(sl >> 3, sp >> 3),
        together(sl & 7, sp & 7),
        together(tl >> 3, tp >> 3),
        together(tl & 7, tp & 7),
        together(leaf_live, par_live),
    ]
    live = parts[4].astype(bf16)
    earlier = mask16(iota((128, 128), 0) < iota((128, 128), 1))
    before = jnp.dot(live, earlier, preferred_element_type=f32)
    place[...] = jnp.where(parts[4] > 0.5, before, 200.0)
    values[...] = jnp.zeros_like(values)
    for q, part in enumerate(parts):
        values[pl.ds(q, 64, stride=8), :] = part
    wanted = iota((128, 128), 0).astype(f32)

    @pl.loop(0, CLASSES, unroll=16)
    def _(k):
        hit = mask16(wanted == place[pl.ds(k, 1), :])
        rows = pl.ds(pl.multiple_of(k * 8, 8), 8)
        packed[rows, :] = dot_nt(values[rows, :].astype(bf16), hit)

    ones = jnp.ones((128, 128), bf16)
    count = jnp.dot(live, ones, preferred_element_type=f32)
    count_row = dot_nt(ones[0:16], live)[0:1, :]
    row, column = iota((64, 64), 0), iota((64, 64), 1)
    count_column = count[:, 0:64]
    ahead = mask16(
        (count_row < count_column) | ((count_row == count_column) & (column < row))
    )
    rank = dot_nt(ones[0:16, 0:64], ahead)[0:1, :]
    perm = mask16(rank == row.astype(f32))

    def sort(v):
        return jnp.dot(perm, v.astype(bf16), preferred_element_type=f32)

    s_high, s_low, t_high, t_low, used = (
        sort(packed[pl.ds(q, 64, stride=8), :]) for q in range(5)
    )
    order = sort(iota((64, 128), 0).astype(f32))
    lane = iota((64, 128), 1)
    source = (s_high * 8 + s_low) * 8
    target = jnp.where(used > 0.5, t_high * 8 + t_low, float(ROWS)) * 8
    idx[0, 0:64, :] = jnp.where(lane == 120, order, source).astype(jnp.int32)
    idx[1, 0:64, :] = target.astype(jnp.int32)
    fits = mask16(count <= (16 * lane).astype(f32))
    pairs = jnp.dot(ones[0:16, 0:64], fits, preferred_element_type=f32)[0:8]
    idx[0, 64:72, :] = pairs.astype(jnp.int32) >> 1
    idx[1, 64:72, :] = jnp.zeros((8, 128), jnp.int32)


def exchange_kernel(
    mp, m2m, lt_in, ls_in, pt_in, ps_in, rem, par, idx_out,
    own, ops, par_own, lt, ls, pt, ps, values, place, packed, idx,
    send, recv, psend, precv, local,
):
    staged = [
        pltpu.make_async_copy(src, dst, local.at[n])
        for n, (src, dst) in enumerate(
            ((mp, own), (m2m, ops), (lt_in, lt), (ls_in, ls), (pt_in, pt), (ps_in, ps))
        )
    ]
    for copy in staged:
        copy.start()
    entry_barrier()
    leaves = Spread(mp, rem, 2, send, recv)
    leaves.start()
    for copy in staged:
        copy.wait()

    row = iota((128, 128), 0)
    select = mask16(iota((128, 128), 1) == 8 * (row & 15) + (row >> 4))
    by_octant = [dot_nt(select, own[c]).astype(bf16) for c in range(3)]
    total = jnp.zeros((48, P_SIZE), f32)
    for o in range(8):
        rows = jnp.concatenate([by_octant[c][16 * o : 16 * o + 16] for c in range(3)], axis=0)
        total = total + jnp.dot(rows, ops[o], preferred_element_type=f32)
    pieces = []
    for c in range(3):
        part = total[16 * c : 16 * c + 16]
        for q in range(2):
            par_own[2 * c + q] = part[:, 128 * q : 128 * q + 128].astype(bf16)
        pieces.append(jnp.concatenate([part[:, 256:296], jnp.zeros((16, 88), f32)], axis=1))
    tails = pieces[0] + pltpu.roll(pieces[1], 40, 1) + pltpu.roll(pieces[2], 80, 1)
    par_own[6] = tails.astype(bf16)
    keep = pltpu.make_async_copy(par_own, par.at[2], local.at[6])
    keep.start()
    parents = Spread(par_own, par, 4, psend, precv)
    parents.start()
    parents.start_unshared()
    leaves.start_unshared()

    leaf_base = (here() - 2) * BOX_DEV
    par_base = (here() - 2) * PAR_DEV - LEAVES
    prepare_lists(ls, lt, ps, pt, leaf_base, par_base, values, place, packed, idx)
    put = pltpu.make_async_copy(idx, idx_out, local.at[7])
    put.start()

    leaves.relay()
    parents.relay()
    keep.wait()
    put.wait()
    leaves.finish()
    parents.finish()


def translate_kernel(
    idx_in, mp, rem, par_in, ops_in, out,
    idx, blocks, par, result, win, g0, g1, o0, o1, ops, ops_sem, sem, *acc,
):
    gathered, terms = (g0, g1), (o0, o1)
    get_idx = pltpu.make_async_copy(idx_in, idx, sem.at[0])
    get_idx.start()
    get_blocks = []
    for j in range(SPAN):
        src = mp if j == 2 else rem.at[j]
        get_blocks.append(pltpu.make_async_copy(src, blocks.at[j], sem.at[1 + j]))
        get_blocks[j].start()
    get_par = pltpu.make_async_copy(par_in, par, sem.at[6])
    get_par.start()

    zeros = jnp.zeros((448, 128), f32)
    for a in acc:

        @pl.loop(0, ACC_ROWS * 8 // 448)
        def _(i):
            a[pl.ds(pl.multiple_of(i * 448, 448), 448), :] = zeros

    for buffer in terms:
        buffer[...] = jnp.zeros_like(buffer)

    get_idx.wait()

    def fetch(r):
        return pltpu.make_async_copy(ops_in.at[idx[0, r, 120]], ops.at[r], ops_sem.at[r])

    @pl.loop(0, CLASSES)
    def _(r):
        fetch(r).start()

    eye = mask16(iota((128, 128), 0) == iota((128, 128), 1))
    get_par.wait()
    for j in range(SPAN):
        get_blocks[j].wait()
        for c in range(3):
            m = dot_nt(eye, blocks[j, c, 0:256, :])
            for q in range(2):
                win[pl.ds(j * 1024 + 2 * c + q, 128, stride=8), :] = m[:, 128 * q : 128 * q + 128]
        tails = jnp.concatenate(
            [blocks[j, c, 256:296, :] for c in range(3)] + [jnp.zeros((8, 128), bf16)], axis=0
        )
        win[pl.ds(j * 1024 + 6, 128, stride=8), :] = dot_nt(eye, tails)
        for r in range(7):
            win[pl.ds((LEAVES + j * 16) * 8 + r, 16, stride=8), :] = par[j, r].astype(f32)

    def at(which, k, s):
        return pl.ds(pl.multiple_of(idx[which, k, s], 8), 8)

    def gather(k, b, n):
        for s in range(n):
            gathered[b][s * 8 : s * 8 + 8, :] = win[at(0, k, s), :]

    def scatter(k, b, n):
        for s in range(n):
            acc[s % CHAINS][at(1, k, s), :] += terms[b][s * 8 : s * 8 + 8, :]

    def multiply(k, b, n):
        rows = [gathered[b][pl.ds(r, n, stride=8), :] for r in range(7)]
        tails = (rows[6], pltpu.roll(rows[6], 88, 1), pltpu.roll(rows[6], 48, 1))
        x = jnp.concatenate(
            [
                jnp.concatenate(
                    [
                        rows[2 * c].astype(bf16),
                        rows[2 * c + 1].astype(bf16),
                        tails[c].astype(bf16)[:, :40],
                    ],
                    axis=1,
                )
                for c in range(3)
            ],
            axis=0,
        )
        y = jnp.dot(x, ops[k], preferred_element_type=f32)
        pieces = []
        for c in range(3):
            part = y[c * n : (c + 1) * n]
            for q in range(2):
                terms[b][pl.ds(2 * c + q, n, stride=8), :] = part[:, 128 * q : 128 * q + 128]
            pieces.append(jnp.concatenate([part[:, 256:296], jnp.zeros((n, 88), f32)], axis=1))
        terms[b][pl.ds(6, n, stride=8), :] = (
            pieces[0] + pltpu.roll(pieces[1], 40, 1) + pltpu.roll(pieces[2], 80, 1)
        )

    start = 0
    for bucket in BUCKETS:
        n = 16 * bucket
        end = idx[0, 64, bucket]

        @pl.when(end > start)
        def _():
            gather(2 * start, 0, n)

        @pl.loop(start, end)
        def _(i):
            k = 2 * i
            fetch(k).wait()
            fetch(k + 1).wait()
            gather(k + 1, 1, n)
            multiply(k, 0, n)
            scatter(jnp.maximum(k - 1, 0), 1, n)
            gather(jnp.minimum(k + 2, CLASSES - 1), 0, n)
            multiply(k + 1, 1, n)
            scatter(k, 0, n)

        start = end
    scatter(CLASSES - 1, 1, SLOTS)

    def total(first, count):
        rows = pl.ds(first, count, stride=8)
        return functools.reduce(lambda p, q: p + q, [a[rows, :] for a in acc])

    puts = []
    for j in range(SPAN):
        for r in range(7):
            leaf = total(j * 1024 + r, 128).astype(bf16)
            result[j, r, 0:128, :] = dot_nt(eye, leaf).astype(bf16)
            result[j, r, 128:144, :] = total(LEAVES * 8 + j * 128 + r, 16).astype(bf16)
        puts.append(pltpu.make_async_copy(result.at[j], out.at[j], sem.at[7 + j]))
        puts[j].start()
    for put in puts:
        put.wait()


def return_kernel(
    partial, side, behind, ahead, mine_near, mine_far, from_near, from_far, send, recv, local
):
    out, out_ok, in_ok = sides()
    first, rest = pl.ds(0, 4), pl.ds(4, 3)
    staged = [
        pltpu.make_async_copy(src, dst, local.at[n])
        for n, (src, dst) in enumerate(
            (
                (partial.at[2 + out, first], mine_near),
                (partial.at[2 - 2 * out, rest], mine_far),
            )
        )
    ]
    for copy in staged:
        copy.start()
    copy = functools.partial(remote, send=send, recv=recv)
    lend_far = copy(partial.at[2 - 2 * out, first], from_near, n=0, offset=-out)
    lend_near = copy(partial.at[2 + out, rest], from_far, n=1, offset=-out)
    to_side = copy(partial.at[2 - out], side, n=2, offset=-out)
    to_far = copy(partial.at[2 + 2 * out], behind, n=3, offset=2 * out)
    sum_near = copy(mine_near, ahead.at[first], n=4, offset=out)
    sum_far = copy(mine_far, ahead.at[rest], n=5, offset=-2 * out)
    entry_barrier()

    @pl.when(in_ok)
    def _():
        lend_far.start()

    @pl.when(out_ok)
    def _():
        lend_near.start()
        to_far.start()

    to_side.start()
    for c in staged:
        c.wait()

    def add(mine, theirs):
        mine[...] = (mine[...].astype(f32) + theirs[...].astype(f32)).astype(bf16)

    @pl.when(out_ok)
    def _():
        lend_far.wait_recv()
        add(mine_near, from_near)
        sum_near.start()

    @pl.when(in_ok)
    def _():
        lend_near.wait_recv()
        add(mine_far, from_far)
        sum_far.start()

    to_side.wait()

    @pl.when(out_ok)
    def _():
        lend_near.wait_send()
        to_far.wait_send()
        sum_near.wait()
        sum_far.wait_recv()

    @pl.when(in_ok)
    def _():
        lend_far.wait_send()
        to_far.wait_recv()
        sum_far.wait_send()


def sum_kernel(partial, side, behind, ahead, leaf, parent, got, leaf_sum, parent_sum, get, put):
    gets = [
        pltpu.make_async_copy(src, got.at[n], get.at[n])
        for n, src in enumerate((partial.at[2], side, behind, ahead))
    ]
    for copy in gets:
        copy.start()
    _, out_ok, in_ok = sides()
    for copy in gets:
        copy.wait()

    def total(r):
        s = got[0, r].astype(f32) + got[1, r].astype(f32)
        s = s + jnp.where(in_ok, got[2, r].astype(f32), 0.0)
        return s + jnp.where(out_ok, got[3, r].astype(f32), 0.0)

    tails = total(6)
    puts = []
    for c in range(3):
        for q in range(2):
            s = total(2 * c + q)
            leaf_sum[c, 128 * q : 128 * q + 128, :] = s[0:128]
            parent_sum[c, :, 128 * q : 128 * q + 128] = s[128:144]
        leaf_sum[c, 256:296, :] = tails[40 * c : 40 * c + 40]
        shifted = tails[128:144] if c == 0 else pltpu.roll(tails[128:144], 128 - 40 * c, 1)
        parent_sum[c, :, 256:296] = shifted[:, :40]
        puts.append(pltpu.make_async_copy(leaf_sum.at[c], leaf.at[c], put.at[c]))
        puts[c].start()
    puts.append(pltpu.make_async_copy(parent_sum, parent, put.at[3]))
    puts[3].start()
    for copy in puts:
        copy.wait()


def on_device(multipole, m2m_ops, m2l_ops, lt, ls, pt, ps):
    mp = jnp.transpose(multipole, (1, 2, 0))
    pt, ps = jnp.transpose(pt[0]), jnp.transpose(ps[0])
    hbm = pl.BlockSpec(memory_space=pltpu.HBM)
    semaphores = pltpu.SemaphoreType.DMA
    rem, par, idx = pl.pallas_call(
        exchange_kernel,
        out_shape=(
            jax.ShapeDtypeStruct((SPAN, 3, P_SIZE, BOX_DEV), bf16),
            jax.ShapeDtypeStruct((SPAN, 7, PAR_DEV, 128), bf16),
            jax.ShapeDtypeStruct((2, 72, 128), jnp.int32),
        ),
        in_specs=[hbm] * 6,
        out_specs=(hbm, hbm, hbm),
        scratch_shapes=[
            pltpu.VMEM((3, P_SIZE, BOX_DEV), bf16),
            pltpu.VMEM((8, P_SIZE, P_SIZE), bf16),
            pltpu.VMEM((7, PAR_DEV, 128), bf16),
            pltpu.VMEM((CLASSES, SLOT), jnp.int32),
            pltpu.VMEM((CLASSES, SLOT), jnp.int32),
            pltpu.VMEM((PSLOT, CLASSES), jnp.int32),
            pltpu.VMEM((PSLOT, CLASSES), jnp.int32),
            pltpu.VMEM((CLASSES * 8, 128), f32),
            pltpu.VMEM((CLASSES, 128), f32),
            pltpu.VMEM((CLASSES * 8, 128), f32),
            pltpu.VMEM((2, 72, 128), jnp.int32),
            semaphores((6,)),
            semaphores((6,)),
            semaphores((6,)),
            semaphores((6,)),
            semaphores((8,)),
        ],
        compiler_params=pltpu.CompilerParams(
            collective_id=0, has_side_effects=True, vmem_limit_bytes=VMEM_BYTES
        ),
        name="exchange",
    )(mp, m2m_ops, lt[0], ls[0], pt, ps)
    partial = pl.pallas_call(
        translate_kernel,
        out_shape=jax.ShapeDtypeStruct((SPAN, 7, BOX_DEV + PAR_DEV, 128), bf16),
        in_specs=[hbm] * 5,
        out_specs=hbm,
        scratch_shapes=[
            pltpu.SMEM((2, 72, 128), jnp.int32),
            pltpu.VMEM((SPAN, 3, P_SIZE, BOX_DEV), bf16),
            pltpu.VMEM((SPAN, 7, PAR_DEV, 128), bf16),
            pltpu.VMEM((SPAN, 7, BOX_DEV + PAR_DEV, 128), bf16),
            pltpu.VMEM((ROWS * 8, 128), f32),
        ]
        + [pltpu.VMEM((SLOTS * 8, 128), f32)] * 4
        + [pltpu.VMEM((CLASSES, P_SIZE, P_SIZE), bf16), semaphores((CLASSES,)), semaphores((12,))]
        + [pltpu.VMEM((ACC_ROWS * 8, 128), f32)] * CHAINS,
        compiler_params=pltpu.CompilerParams(vmem_limit_bytes=VMEM_BYTES),
        name="translate",
    )(idx, mp, rem, par, m2l_ops)
    block = (7, BOX_DEV + PAR_DEV, 128)
    results = (
        jax.ShapeDtypeStruct((3, P_SIZE, BOX_DEV), f32),
        jax.ShapeDtypeStruct((3, PAR_DEV, P_SIZE), f32),
    )
    side, behind, ahead = pl.pallas_call(
        return_kernel,
        out_shape=(jax.ShapeDtypeStruct(block, bf16),) * 3,
        in_specs=[hbm],
        out_specs=(hbm,) * 3,
        scratch_shapes=[
            pltpu.VMEM((4,) + block[1:], bf16),
            pltpu.VMEM((3,) + block[1:], bf16),
            pltpu.VMEM((4,) + block[1:], bf16),
            pltpu.VMEM((3,) + block[1:], bf16),
            semaphores((6,)),
            semaphores((6,)),
            semaphores((2,)),
        ],
        compiler_params=pltpu.CompilerParams(
            collective_id=1, has_side_effects=True, vmem_limit_bytes=VMEM_BYTES
        ),
        name="return",
    )(partial)
    leaf, parent = pl.pallas_call(
        sum_kernel,
        out_shape=results,
        in_specs=[hbm] * 4,
        out_specs=(hbm, hbm),
        scratch_shapes=[
            pltpu.VMEM((4,) + block, bf16),
            pltpu.VMEM((3, P_SIZE, BOX_DEV), f32),
            pltpu.VMEM((3, PAR_DEV, P_SIZE), f32),
            semaphores((4,)),
            semaphores((4,)),
        ],
        compiler_params=pltpu.CompilerParams(vmem_limit_bytes=VMEM_BYTES),
        name="sums",
    )(partial, side, behind, ahead)
    return jnp.transpose(leaf, (2, 0, 1)), jnp.transpose(parent, (1, 0, 2))


def solution(mesh):
    boxes = P(("gx", "gy"), None, None)
    return jax.shard_map(
        on_device,
        mesh=mesh,
        in_specs=(boxes, P(), P(), boxes, boxes, boxes, boxes),
        out_specs=(boxes, boxes),
        check_vma=False,
    )
```

```python
import functools

import jax
import jax.numpy as jnp
from jax import lax
from jax.experimental import pallas as pl
from jax.experimental.pallas import tpu as pltpu
from jax.sharding import PartitionSpec as P

CLASSES = 64
SLOT = 80
PSLOT = 32
BUCKETS = (3, 4, 5, 6, 7)
STEP = 4
SLOTS = SLOT + PSLOT
P_SIZE = 296
BOX_DEV = 128
PAR_DEV = 16
SPAN = 5
LEAVES = SPAN * BOX_DEV
ROWS = LEAVES + SPAN * PAR_DEV
ACC_ROWS = ROWS + 8
CHAINS = 4
DEVICES = 128
VMEM_BYTES = 63 * 1024 * 1024
N_GY = 8
MESH = pl.DeviceIdType.MESH
f32 = jnp.float32
bf16 = jnp.bfloat16


def dot_nt(a, b):
    return lax.dot_general(a, b, (((1,), (1,)), ((), ())), preferred_element_type=f32)


def mask16(x):
    return x.astype(f32).astype(bf16)


def iota(shape, dim):
    return lax.broadcasted_iota(jnp.int32, shape, dim)


def here():
    return lax.axis_index("gx") * N_GY + lax.axis_index("gy")


def device_at(offset):
    index = lax.rem(here() + (offset + DEVICES), DEVICES)
    return (lax.div(index, N_GY), lax.rem(index, N_GY))


def sides():
    me = here()
    out = 2 * lax.rem(me, 2) - 1
    ahead, behind = me + 2 * out, me - 2 * out
    return out, (ahead >= 0) & (ahead < DEVICES), (behind >= 0) & (behind < DEVICES)


def entry_barrier():
    barrier = pltpu.get_barrier_semaphore()
    out, out_ok, in_ok = sides()

    def greet(offset):
        pl.semaphore_signal(barrier, inc=1, device_id=device_at(offset), device_id_type=MESH)

    greet(-out)

    @pl.when(out_ok)
    def _():
        greet(out)
        greet(2 * out)

    @pl.when(in_ok)
    def _():
        greet(-2 * out)

    pl.semaphore_wait(barrier, 1 + 2 * out_ok.astype(jnp.int32) + in_ok.astype(jnp.int32))


def remote(src, dst, send, recv, n, offset):
    return pltpu.make_async_remote_copy(
        src_ref=src,
        dst_ref=dst,
        send_sem=send.at[n],
        recv_sem=recv.at[n],
        device_id=device_at(offset),
        device_id_type=MESH,
    )


class Spread:
    def __init__(self, own, blocks, cut, send, recv):
        out, self.out_ok, self.in_ok = sides()
        first, rest = pl.ds(0, cut), pl.ds(cut, own.shape[0] - cut)
        copy = functools.partial(remote, send=send, recv=recv)
        self.sibling = copy(own, blocks.at[2 + out], n=0, offset=-out)
        self.behind = copy(own, blocks.at[2 + 2 * out], n=1, offset=-2 * out)
        self.near = copy(own.at[first], blocks.at[2 - out, first], n=2, offset=out)
        self.far = copy(own.at[rest], blocks.at[2 - 2 * out, rest], n=3, offset=2 * out)
        self.relay_near = copy(
            blocks.at[2 + out, first], blocks.at[2 + 2 * out, first], n=4, offset=-out
        )
        self.relay_far = copy(
            blocks.at[2 - 2 * out, rest], blocks.at[2 - out, rest], n=5, offset=-out
        )

    def start(self):
        @pl.when(self.out_ok)
        def _():
            self.near.start()
            self.far.start()

        @pl.when(self.in_ok)
        def _():
            self.behind.start()

        self.sibling.start()

    def relay(self):
        @pl.when(self.out_ok)
        def _():
            self.near.wait_recv()
            self.relay_near.start()

        @pl.when(self.in_ok)
        def _():
            self.far.wait_recv()
            self.relay_far.start()

    def finish(self):
        self.sibling.wait()

        @pl.when(self.out_ok)
        def _():
            self.near.wait_send()
            self.far.wait_send()
            self.behind.wait_recv()
            self.relay_near.wait_send()
            self.relay_far.wait_recv()

        @pl.when(self.in_ok)
        def _():
            self.behind.wait_send()
            self.relay_far.wait_send()
            self.relay_near.wait_recv()


def prepare_lists(ls, lt, ps, pt, leaf_base, par_base, values, place, packed, idx):
    eye = mask16(iota((64, 64), 0) == iota((64, 64), 1))

    def together(leaf, parent):
        low = jnp.concatenate(
            [jnp.zeros((80, 64), bf16), mask16(parent), jnp.zeros((16, 64), bf16)], axis=0
        )
        high = jnp.concatenate([leaf.astype(f32), jnp.zeros((64, 48), f32)], axis=1)
        return high + dot_nt(eye, low)

    leaf_live, par_live = ls[...] >= 0, ps[...] >= 0
    sl = jnp.where(leaf_live, ls[...] - leaf_base, 0)
    tl = jnp.where(leaf_live, lt[...] - leaf_base, 0)
    sp = jnp.where(par_live, ps[...] - par_base, 0)
    tp = jnp.where(par_live, pt[...] - par_base, 0)
    parts = [
        together(sl >> 3, sp >> 3),
        together(sl & 7, sp & 7),
        together(tl >> 3, tp >> 3),
        together(tl & 7, tp & 7),
        together(leaf_live, par_live),
    ]
    live = parts[4].astype(bf16)
    earlier = mask16(iota((128, 128), 0) < iota((128, 128), 1))
    before = jnp.dot(live, earlier, preferred_element_type=f32)
    place[...] = jnp.where(parts[4] > 0.5, before, 200.0)
    values[...] = jnp.zeros_like(values)
    for q, part in enumerate(parts):
        values[pl.ds(q, 64, stride=8), :] = part
    wanted = iota((128, 128), 0).astype(f32)

    @pl.loop(0, CLASSES, unroll=16)
    def _(k):
        hit = mask16(wanted == place[pl.ds(k, 1), :])
        rows = pl.ds(pl.multiple_of(k * 8, 8), 8)
        packed[rows, :] = dot_nt(values[rows, :].astype(bf16), hit)

    ones = jnp.ones((128, 128), bf16)
    count = jnp.dot(live, ones, preferred_element_type=f32)
    count_row = dot_nt(ones[0:16], live)[0:1, :]
    row, column = iota((64, 64), 0), iota((64, 64), 1)
    count_column = count[:, 0:64]
    ahead = mask16(
        (count_row < count_column) | ((count_row == count_column) & (column < row))
    )
    rank = dot_nt(ones[0:16, 0:64], ahead)[0:1, :]
    perm = mask16(rank == row.astype(f32))

    def sort(v):
        return jnp.dot(perm, v.astype(bf16), preferred_element_type=f32)

    s_high, s_low, t_high, t_low, used = (
        sort(packed[pl.ds(q, 64, stride=8), :]) for q in range(5)
    )
    order = sort(iota((64, 128), 0).astype(f32))
    lane = iota((64, 128), 1)
    source = (s_high * 8 + s_low) * 8
    target = jnp.where(used > 0.5, t_high * 8 + t_low, float(ROWS)) * 8
    idx[0, 0:64, :] = jnp.where(lane == 120, order, source).astype(jnp.int32)
    idx[1, 0:64, :] = target.astype(jnp.int32)
    fits = mask16(count <= (16 * lane).astype(f32))
    groups = jnp.dot(ones[0:16, 0:64], fits, preferred_element_type=f32)[0:8]
    idx[0, 64:72, :] = groups.astype(jnp.int32) // STEP
    idx[1, 64:72, :] = jnp.zeros((8, 128), jnp.int32)


def exchange_kernel(
    mp, m2m, lt_in, ls_in, pt_in, ps_in, rem, par, idx_out,
    own, ops, par_own, lt, ls, pt, ps, values, place, packed, idx,
    send, recv, psend, precv, local,
):
    staged = [
        pltpu.make_async_copy(src, dst, local.at[n])
        for n, (src, dst) in enumerate(
            ((mp, own), (m2m, ops), (lt_in, lt), (ls_in, ls), (pt_in, pt), (ps_in, ps))
        )
    ]
    for copy in staged:
        copy.start()
    entry_barrier()
    leaves = Spread(mp, rem, 2, send, recv)
    leaves.start()
    for copy in staged:
        copy.wait()

    row = iota((128, 128), 0)
    select = mask16(iota((128, 128), 1) == 8 * (row & 15) + (row >> 4))
    by_octant = [dot_nt(select, own[c]).astype(bf16) for c in range(3)]
    total = jnp.zeros((48, P_SIZE), f32)
    for o in range(8):
        rows = jnp.concatenate([by_octant[c][16 * o : 16 * o + 16] for c in range(3)], axis=0)
        total = total + jnp.dot(rows, ops[o], preferred_element_type=f32)
    pieces = []
    for c in range(3):
        part = total[16 * c : 16 * c + 16]
        for q in range(2):
            par_own[2 * c + q] = part[:, 128 * q : 128 * q + 128].astype(bf16)
        pieces.append(jnp.concatenate([part[:, 256:296], jnp.zeros((16, 88), f32)], axis=1))
    tails = pieces[0] + pltpu.roll(pieces[1], 40, 1) + pltpu.roll(pieces[2], 80, 1)
    par_own[6] = tails.astype(bf16)
    keep = pltpu.make_async_copy(par_own, par.at[2], local.at[6])
    keep.start()
    parents = Spread(par_own, par, 4, psend, precv)
    parents.start()

    leaf_base = (here() - 2) * BOX_DEV
    par_base = (here() - 2) * PAR_DEV - LEAVES
    prepare_lists(ls, lt, ps, pt, leaf_base, par_base, values, place, packed, idx)
    put = pltpu.make_async_copy(idx, idx_out, local.at[7])
    put.start()

    leaves.relay()
    parents.relay()
    keep.wait()
    put.wait()
    leaves.finish()
    parents.finish()


def translate_kernel(
    idx_in, mp, rem, par_in, ops_in, out,
    idx, blocks, par, result, win, g0, g1, o0, o1, ops, ops_sem, sem, *acc,
):
    gathered, terms = (g0, g1), (o0, o1)
    get_idx = pltpu.make_async_copy(idx_in, idx, sem.at[0])
    get_idx.start()
    get_blocks = []
    for j in range(SPAN):
        src = mp if j == 2 else rem.at[j]
        get_blocks.append(pltpu.make_async_copy(src, blocks.at[j], sem.at[1 + j]))
        get_blocks[j].start()
    get_par = pltpu.make_async_copy(par_in, par, sem.at[6])
    get_par.start()

    zeros = jnp.zeros((448, 128), f32)
    for a in acc:

        @pl.loop(0, ACC_ROWS * 8 // 448)
        def _(i):
            a[pl.ds(pl.multiple_of(i * 448, 448), 448), :] = zeros

    for buffer in terms:
        buffer[...] = jnp.zeros_like(buffer)

    get_idx.wait()

    def fetch(r):
        return pltpu.make_async_copy(ops_in.at[idx[0, r, 120]], ops.at[r], ops_sem.at[r])

    @pl.loop(0, CLASSES)
    def _(r):
        fetch(r).start()

    eye = mask16(iota((128, 128), 0) == iota((128, 128), 1))
    get_par.wait()
    for j in range(SPAN):
        get_blocks[j].wait()
        for c in range(3):
            m = dot_nt(eye, blocks[j, c, 0:256, :])
            for q in range(2):
                win[pl.ds(j * 1024 + 2 * c + q, 128, stride=8), :] = m[:, 128 * q : 128 * q + 128]
        tails = jnp.concatenate(
            [blocks[j, c, 256:296, :] for c in range(3)] + [jnp.zeros((8, 128), bf16)], axis=0
        )
        win[pl.ds(j * 1024 + 6, 128, stride=8), :] = dot_nt(eye, tails)
        for r in range(7):
            win[pl.ds((LEAVES + j * 16) * 8 + r, 16, stride=8), :] = par[j, r].astype(f32)

    def at(which, k, s):
        return pl.ds(pl.multiple_of(idx[which, k, s], 8), 8)

    def gather(k, b, n):
        for s in range(n):
            gathered[b][s * 8 : s * 8 + 8, :] = win[at(0, k, s), :]

    def scatter(k, b, n):
        for s in range(n):
            acc[s % CHAINS][at(1, k, s), :] += terms[b][s * 8 : s * 8 + 8, :]

    def multiply(k, b, n):
        rows = [gathered[b][pl.ds(r, n, stride=8), :] for r in range(7)]
        tails = (rows[6], pltpu.roll(rows[6], 88, 1), pltpu.roll(rows[6], 48, 1))
        x = jnp.concatenate(
            [
                jnp.concatenate(
                    [
                        rows[2 * c].astype(bf16),
                        rows[2 * c + 1].astype(bf16),
                        tails[c].astype(bf16)[:, :40],
                    ],
                    axis=1,
                )
                for c in range(3)
            ],
            axis=0,
        )
        y = jnp.dot(x, ops[k], preferred_element_type=f32)
        pieces = []
        for c in range(3):
            part = y[c * n : (c + 1) * n]
            for q in range(2):
                terms[b][pl.ds(2 * c + q, n, stride=8), :] = part[:, 128 * q : 128 * q + 128]
            pieces.append(jnp.concatenate([part[:, 256:296], jnp.zeros((n, 88), f32)], axis=1))
        terms[b][pl.ds(6, n, stride=8), :] = (
            pieces[0] + pltpu.roll(pieces[1], 40, 1) + pltpu.roll(pieces[2], 80, 1)
        )

    start = 0
    for bucket in BUCKETS:
        n = 16 * bucket
        end = idx[0, 64, bucket]

        @pl.when(end > start)
        def _():
            gather(STEP * start, 0, n)

        @pl.loop(start, end)
        def _(i):
            first = STEP * i
            for u in range(STEP):
                fetch(first + u).wait()
            for u in range(STEP):
                k, now, other = first + u, u % 2, 1 - u % 2
                gather(k + 1 if u < STEP - 1 else jnp.minimum(k + 1, CLASSES - 1), other, n)
                multiply(k, now, n)
                scatter(k - 1 if u else jnp.maximum(k - 1, 0), other, n)

        start = end
    scatter(CLASSES - 1, 1, SLOTS)

    def merge(first, count):
        rows = pl.ds(first, count)
        win[rows, :] = functools.reduce(lambda p, q: p + q, [a[rows, :] for a in acc])

    puts = []
    for j in range(SPAN):
        leaf, parent = j * 1024, LEAVES * 8 + j * 128
        merge(leaf, 1024)
        merge(parent, 128)
        for r in range(7):
            rows = win[pl.ds(leaf + r, 128, stride=8), :].astype(bf16)
            result[j, r, 0:128, :] = dot_nt(eye, rows).astype(bf16)
            result[j, r, 128:144, :] = win[pl.ds(parent + r, 16, stride=8), :].astype(bf16)
        puts.append(pltpu.make_async_copy(result.at[j], out.at[j], sem.at[7 + j]))
        puts[j].start()
    for put in puts:
        put.wait()


def return_kernel(
    partial, side, behind, ahead, mine_near, mine_far, from_near, from_far, send, recv, local
):
    out, out_ok, in_ok = sides()
    first, rest = pl.ds(0, 4), pl.ds(4, 3)
    staged = [
        pltpu.make_async_copy(src, dst, local.at[n])
        for n, (src, dst) in enumerate(
            (
                (partial.at[2 + out, first], mine_near),
                (partial.at[2 - 2 * out, rest], mine_far),
            )
        )
    ]
    for copy in staged:
        copy.start()
    copy = functools.partial(remote, send=send, recv=recv)
    lend_far = copy(partial.at[2 - 2 * out, first], from_near, n=0, offset=-out)
    lend_near = copy(partial.at[2 + out, rest], from_far, n=1, offset=-out)
    to_side = copy(partial.at[2 - out], side, n=2, offset=-out)
    to_far = copy(partial.at[2 + 2 * out], behind, n=3, offset=2 * out)
    sum_near = copy(mine_near, ahead.at[first], n=4, offset=out)
    sum_far = copy(mine_far, ahead.at[rest], n=5, offset=-2 * out)
    entry_barrier()

    @pl.when(in_ok)
    def _():
        lend_far.start()

    @pl.when(out_ok)
    def _():
        lend_near.start()
        to_far.start()

    to_side.start()
    for c in staged:
        c.wait()

    def add(mine, theirs):
        mine[...] = (mine[...].astype(f32) + theirs[...].astype(f32)).astype(bf16)

    @pl.when(out_ok)
    def _():
        lend_far.wait_recv()
        add(mine_near, from_near)
        sum_near.start()

    @pl.when(in_ok)
    def _():
        lend_near.wait_recv()
        add(mine_far, from_far)
        sum_far.start()

    to_side.wait()

    @pl.when(out_ok)
    def _():
        lend_near.wait_send()
        to_far.wait_send()
        sum_near.wait()
        sum_far.wait_recv()

    @pl.when(in_ok)
    def _():
        lend_far.wait_send()
        to_far.wait_recv()
        sum_far.wait_send()


def sum_kernel(partial, side, behind, ahead, leaf, parent, got, leaf_sum, parent_sum, get, put):
    pieces = (pl.ds(6, 1), pl.ds(0, 2), pl.ds(2, 2), pl.ds(4, 2))
    gets = [
        [
            pltpu.make_async_copy(src.at[rows], got.at[n, rows], get.at[4 * p + n])
            for n, src in enumerate((partial.at[2], side, behind, ahead))
        ]
        for p, rows in enumerate(pieces)
    ]
    for piece in gets:
        for copy in piece:
            copy.start()
    _, out_ok, in_ok = sides()

    def total(r):
        s = got[0, r].astype(f32) + got[1, r].astype(f32)
        s = s + jnp.where(in_ok, got[2, r].astype(f32), 0.0)
        return s + jnp.where(out_ok, got[3, r].astype(f32), 0.0)

    for copy in gets[0]:
        copy.wait()
    tails = total(6)
    puts = []
    for c in range(3):
        for copy in gets[1 + c]:
            copy.wait()
        for q in range(2):
            s = total(2 * c + q)
            leaf_sum[c, 128 * q : 128 * q + 128, :] = s[0:128]
            parent_sum[c, :, 128 * q : 128 * q + 128] = s[128:144]
        leaf_sum[c, 256:296, :] = tails[40 * c : 40 * c + 40]
        shifted = tails[128:144] if c == 0 else pltpu.roll(tails[128:144], 128 - 40 * c, 1)
        parent_sum[c, :, 256:296] = shifted[:, :40]
        puts.append(pltpu.make_async_copy(leaf_sum.at[c], leaf.at[c], put.at[c]))
        puts[c].start()
    puts.append(pltpu.make_async_copy(parent_sum, parent, put.at[3]))
    puts[3].start()
    for copy in puts:
        copy.wait()


def on_device(multipole, m2m_ops, m2l_ops, lt, ls, pt, ps):
    mp = jnp.transpose(multipole, (1, 2, 0))
    pt, ps = jnp.transpose(pt[0]), jnp.transpose(ps[0])
    hbm = pl.BlockSpec(memory_space=pltpu.HBM)
    semaphores = pltpu.SemaphoreType.DMA
    rem, par, idx = pl.pallas_call(
        exchange_kernel,
        out_shape=(
            jax.ShapeDtypeStruct((SPAN, 3, P_SIZE, BOX_DEV), bf16),
            jax.ShapeDtypeStruct((SPAN, 7, PAR_DEV, 128), bf16),
            jax.ShapeDtypeStruct((2, 72, 128), jnp.int32),
        ),
        in_specs=[hbm] * 6,
        out_specs=(hbm, hbm, hbm),
        scratch_shapes=[
            pltpu.VMEM((3, P_SIZE, BOX_DEV), bf16),
            pltpu.VMEM((8, P_SIZE, P_SIZE), bf16),
            pltpu.VMEM((7, PAR_DEV, 128), bf16),
            pltpu.VMEM((CLASSES, SLOT), jnp.int32),
            pltpu.VMEM((CLASSES, SLOT), jnp.int32),
            pltpu.VMEM((PSLOT, CLASSES), jnp.int32),
            pltpu.VMEM((PSLOT, CLASSES), jnp.int32),
            pltpu.VMEM((CLASSES * 8, 128), f32),
            pltpu.VMEM((CLASSES, 128), f32),
            pltpu.VMEM((CLASSES * 8, 128), f32),
            pltpu.VMEM((2, 72, 128), jnp.int32),
            semaphores((6,)),
            semaphores((6,)),
            semaphores((6,)),
            semaphores((6,)),
            semaphores((8,)),
        ],
        compiler_params=pltpu.CompilerParams(
            collective_id=0, has_side_effects=True, vmem_limit_bytes=VMEM_BYTES
        ),
        name="exchange",
    )(mp, m2m_ops, lt[0], ls[0], pt, ps)
    partial = pl.pallas_call(
        translate_kernel,
        out_shape=jax.ShapeDtypeStruct((SPAN, 7, BOX_DEV + PAR_DEV, 128), bf16),
        in_specs=[hbm] * 5,
        out_specs=hbm,
        scratch_shapes=[
            pltpu.SMEM((2, 72, 128), jnp.int32),
            pltpu.VMEM((SPAN, 3, P_SIZE, BOX_DEV), bf16),
            pltpu.VMEM((SPAN, 7, PAR_DEV, 128), bf16),
            pltpu.VMEM((SPAN, 7, BOX_DEV + PAR_DEV, 128), bf16),
            pltpu.VMEM((ROWS * 8, 128), f32),
        ]
        + [pltpu.VMEM((SLOTS * 8, 128), f32)] * 4
        + [pltpu.VMEM((CLASSES, P_SIZE, P_SIZE), bf16), semaphores((CLASSES,)), semaphores((12,))]
        + [pltpu.VMEM((ACC_ROWS * 8, 128), f32)] * CHAINS,
        compiler_params=pltpu.CompilerParams(vmem_limit_bytes=VMEM_BYTES),
        name="translate",
    )(idx, mp, rem, par, m2l_ops)
    block = (7, BOX_DEV + PAR_DEV, 128)
    results = (
        jax.ShapeDtypeStruct((3, P_SIZE, BOX_DEV), f32),
        jax.ShapeDtypeStruct((3, PAR_DEV, P_SIZE), f32),
    )
    side, behind, ahead = pl.pallas_call(
        return_kernel,
        out_shape=(jax.ShapeDtypeStruct(block, bf16),) * 3,
        in_specs=[hbm],
        out_specs=(hbm,) * 3,
        scratch_shapes=[
            pltpu.VMEM((4,) + block[1:], bf16),
            pltpu.VMEM((3,) + block[1:], bf16),
            pltpu.VMEM((4,) + block[1:], bf16),
            pltpu.VMEM((3,) + block[1:], bf16),
            semaphores((6,)),
            semaphores((6,)),
            semaphores((2,)),
        ],
        compiler_params=pltpu.CompilerParams(
            collective_id=1, has_side_effects=True, vmem_limit_bytes=VMEM_BYTES
        ),
        name="return",
    )(partial)
    leaf, parent = pl.pallas_call(
        sum_kernel,
        out_shape=results,
        in_specs=[hbm] * 4,
        out_specs=(hbm, hbm),
        scratch_shapes=[
            pltpu.VMEM((4,) + block, bf16),
            pltpu.VMEM((3, P_SIZE, BOX_DEV), f32),
            pltpu.VMEM((3, PAR_DEV, P_SIZE), f32),
            semaphores((16,)),
            semaphores((4,)),
        ],
        compiler_params=pltpu.CompilerParams(vmem_limit_bytes=VMEM_BYTES),
        name="sums",
    )(partial, side, behind, ahead)
    return jnp.transpose(leaf, (2, 0, 1)), jnp.transpose(parent, (1, 0, 2))


def solution(mesh):
    boxes = P(("gx", "gy"), None, None)
    return jax.shard_map(
        on_device,
        mesh=mesh,
        in_specs=(boxes, P(), P(), boxes, boxes, boxes, boxes),
        out_specs=(boxes, boxes),
        check_vma=False,
    )
```

```python
import functools

import jax
import jax.numpy as jnp
from jax import lax
from jax.experimental import pallas as pl
from jax.experimental.pallas import tpu as pltpu
from jax.sharding import PartitionSpec as P

CLASSES = 64
SLOT = 80
PSLOT = 32
BUCKETS = (3, 4, 5, 6, 7)
STEP = 4
SLOTS = SLOT + PSLOT
P_SIZE = 296
BOX_DEV = 128
PAR_DEV = 16
SPAN = 5
LEAVES = SPAN * BOX_DEV
ROWS = LEAVES + SPAN * PAR_DEV
ACC_ROWS = ROWS + 8
CHAINS = 4
DEVICES = 128
VMEM_BYTES = 63 * 1024 * 1024
N_GY = 8
MESH = pl.DeviceIdType.MESH
f32 = jnp.float32
bf16 = jnp.bfloat16


def dot_nt(a, b):
    return lax.dot_general(a, b, (((1,), (1,)), ((), ())), preferred_element_type=f32)


def mask16(x):
    return x.astype(f32).astype(bf16)


def iota(shape, dim):
    return lax.broadcasted_iota(jnp.int32, shape, dim)


def here():
    return lax.axis_index("gx") * N_GY + lax.axis_index("gy")


def device_at(offset):
    index = lax.rem(here() + (offset + DEVICES), DEVICES)
    return (lax.div(index, N_GY), lax.rem(index, N_GY))


def sides():
    me = here()
    out = 2 * lax.rem(me, 2) - 1
    ahead, behind = me + 2 * out, me - 2 * out
    return out, (ahead >= 0) & (ahead < DEVICES), (behind >= 0) & (behind < DEVICES)


def greet():
    barrier = pltpu.get_barrier_semaphore()
    out, out_ok, in_ok = sides()

    def signal(offset):
        pl.semaphore_signal(barrier, inc=1, device_id=device_at(offset), device_id_type=MESH)

    signal(-out)

    @pl.when(out_ok)
    def _():
        signal(out)
        signal(2 * out)

    @pl.when(in_ok)
    def _():
        signal(-2 * out)


def await_greetings():
    _, out_ok, in_ok = sides()
    peers = 1 + 2 * out_ok.astype(jnp.int32) + in_ok.astype(jnp.int32)
    pl.semaphore_wait(pltpu.get_barrier_semaphore(), peers)


def remote(src, dst, send, recv, n, offset):
    return pltpu.make_async_remote_copy(
        src_ref=src,
        dst_ref=dst,
        send_sem=send.at[n],
        recv_sem=recv.at[n],
        device_id=device_at(offset),
        device_id_type=MESH,
    )


class Spread:
    def __init__(self, own, blocks, cut, send, recv):
        out, self.out_ok, self.in_ok = sides()
        first, rest = pl.ds(0, cut), pl.ds(cut, own.shape[0] - cut)
        copy = functools.partial(remote, send=send, recv=recv)
        self.sibling = copy(own, blocks.at[2 + out], n=0, offset=-out)
        self.behind = copy(own, blocks.at[2 + 2 * out], n=1, offset=-2 * out)
        self.near = copy(own.at[first], blocks.at[2 - out, first], n=2, offset=out)
        self.far = copy(own.at[rest], blocks.at[2 - 2 * out, rest], n=3, offset=2 * out)
        self.relay_near = copy(
            blocks.at[2 + out, first], blocks.at[2 + 2 * out, first], n=4, offset=-out
        )
        self.relay_far = copy(
            blocks.at[2 - 2 * out, rest], blocks.at[2 - out, rest], n=5, offset=-out
        )

    def start(self):
        @pl.when(self.out_ok)
        def _():
            self.near.start()
            self.far.start()

        @pl.when(self.in_ok)
        def _():
            self.behind.start()

        self.sibling.start()

    def relay(self):
        @pl.when(self.out_ok)
        def _():
            self.near.wait_recv()
            self.relay_near.start()

        @pl.when(self.in_ok)
        def _():
            self.far.wait_recv()
            self.relay_far.start()

    def finish(self):
        self.sibling.wait()

        @pl.when(self.out_ok)
        def _():
            self.near.wait_send()
            self.far.wait_send()
            self.behind.wait_recv()
            self.relay_near.wait_send()
            self.relay_far.wait_recv()

        @pl.when(self.in_ok)
        def _():
            self.behind.wait_send()
            self.relay_far.wait_send()
            self.relay_near.wait_recv()


def prepare_lists(ls, lt, ps, pt, leaf_base, par_base, values, place, packed, idx):
    eye = mask16(iota((64, 64), 0) == iota((64, 64), 1))

    def together(leaf, parent):
        low = jnp.concatenate(
            [jnp.zeros((80, 64), bf16), mask16(parent), jnp.zeros((16, 64), bf16)], axis=0
        )
        high = jnp.concatenate([leaf.astype(f32), jnp.zeros((64, 48), f32)], axis=1)
        return high + dot_nt(eye, low)

    leaf_live, par_live = ls[...] >= 0, ps[...] >= 0
    sl = jnp.where(leaf_live, ls[...] - leaf_base, 0)
    tl = jnp.where(leaf_live, lt[...] - leaf_base, 0)
    sp = jnp.where(par_live, ps[...] - par_base, 0)
    tp = jnp.where(par_live, pt[...] - par_base, 0)
    parts = [
        together(sl >> 3, sp >> 3),
        together(sl & 7, sp & 7),
        together(tl >> 3, tp >> 3),
        together(tl & 7, tp & 7),
        together(leaf_live, par_live),
    ]
    live = parts[4].astype(bf16)
    earlier = mask16(iota((128, 128), 0) < iota((128, 128), 1))
    before = jnp.dot(live, earlier, preferred_element_type=f32)
    place[...] = jnp.where(parts[4] > 0.5, before, 200.0)
    values[...] = jnp.zeros_like(values)
    for q, part in enumerate(parts):
        values[pl.ds(q, 64, stride=8), :] = part
    wanted = iota((128, 128), 0).astype(f32)

    @pl.loop(0, CLASSES, unroll=16)
    def _(k):
        hit = mask16(wanted == place[pl.ds(k, 1), :])
        rows = pl.ds(pl.multiple_of(k * 8, 8), 8)
        packed[rows, :] = dot_nt(values[rows, :].astype(bf16), hit)

    ones = jnp.ones((128, 128), bf16)
    count = jnp.dot(live, ones, preferred_element_type=f32)
    count_row = dot_nt(ones[0:16], live)[0:1, :]
    row, column = iota((64, 64), 0), iota((64, 64), 1)
    count_column = count[:, 0:64]
    ahead = mask16(
        (count_row < count_column) | ((count_row == count_column) & (column < row))
    )
    rank = dot_nt(ones[0:16, 0:64], ahead)[0:1, :]
    perm = mask16(rank == row.astype(f32))

    def sort(v):
        return jnp.dot(perm, v.astype(bf16), preferred_element_type=f32)

    s_high, s_low, t_high, t_low, used = (
        sort(packed[pl.ds(q, 64, stride=8), :]) for q in range(5)
    )
    order = sort(iota((64, 128), 0).astype(f32))
    lane = iota((64, 128), 1)
    source = (s_high * 8 + s_low) * 8
    target = jnp.where(used > 0.5, t_high * 8 + t_low, float(ROWS)) * 8
    idx[0, 0:64, :] = jnp.where(lane == 120, order, source).astype(jnp.int32)
    idx[1, 0:64, :] = target.astype(jnp.int32)
    fits = mask16(count <= (16 * lane).astype(f32))
    groups = jnp.dot(ones[0:16, 0:64], fits, preferred_element_type=f32)[0:8]
    idx[0, 64:72, :] = groups.astype(jnp.int32) // STEP
    idx[1, 64:72, :] = jnp.zeros((8, 128), jnp.int32)


def exchange_kernel(
    mp, m2m, lt_in, ls_in, pt_in, ps_in, rem, par, idx_out,
    own, ops, par_own, lt, ls, pt, ps, values, place, packed, idx,
    send, recv, psend, precv, local,
):
    staged = [
        pltpu.make_async_copy(src, dst, local.at[n])
        for n, (src, dst) in enumerate(
            ((mp, own), (m2m, ops), (lt_in, lt), (ls_in, ls), (pt_in, pt), (ps_in, ps))
        )
    ]
    for copy in staged:
        copy.start()
    greet()
    for copy in staged:
        copy.wait()

    row = iota((128, 128), 0)
    select = mask16(iota((128, 128), 1) == 8 * (row & 15) + (row >> 4))
    by_octant = [dot_nt(select, own[c]).astype(bf16) for c in range(3)]
    total = jnp.zeros((48, P_SIZE), f32)
    for o in range(8):
        rows = jnp.concatenate([by_octant[c][16 * o : 16 * o + 16] for c in range(3)], axis=0)
        total = total + jnp.dot(rows, ops[o], preferred_element_type=f32)
    pieces = []
    for c in range(3):
        part = total[16 * c : 16 * c + 16]
        for q in range(2):
            par_own[2 * c + q] = part[:, 128 * q : 128 * q + 128].astype(bf16)
        pieces.append(jnp.concatenate([part[:, 256:296], jnp.zeros((16, 88), f32)], axis=1))
    tails = pieces[0] + pltpu.roll(pieces[1], 40, 1) + pltpu.roll(pieces[2], 80, 1)
    par_own[6] = tails.astype(bf16)
    await_greetings()
    parents = Spread(par_own, par, 4, psend, precv)
    leaves = Spread(mp, rem, 2, send, recv)
    parents.start()
    leaves.start()
    keep = pltpu.make_async_copy(par_own, par.at[2], local.at[6])
    keep.start()

    leaf_base = (here() - 2) * BOX_DEV
    par_base = (here() - 2) * PAR_DEV - LEAVES
    prepare_lists(ls, lt, ps, pt, leaf_base, par_base, values, place, packed, idx)
    put = pltpu.make_async_copy(idx, idx_out, local.at[7])
    put.start()

    parents.relay()
    leaves.relay()
    keep.wait()
    put.wait()
    leaves.finish()
    parents.finish()


def translate_kernel(
    idx_in, mp, rem, par_in, ops_in, out,
    idx, blocks, par, result, win, g0, g1, o0, o1, ops, ops_sem, sem, *acc,
):
    gathered, terms = (g0, g1), (o0, o1)
    get_idx = pltpu.make_async_copy(idx_in, idx, sem.at[0])
    get_idx.start()
    get_blocks = []
    for j in range(SPAN):
        src = mp if j == 2 else rem.at[j]
        get_blocks.append(pltpu.make_async_copy(src, blocks.at[j], sem.at[1 + j]))
        get_blocks[j].start()
    get_par = pltpu.make_async_copy(par_in, par, sem.at[6])
    get_par.start()

    zeros = jnp.zeros((448, 128), f32)
    for a in acc:

        @pl.loop(0, ACC_ROWS * 8 // 448)
        def _(i):
            a[pl.ds(pl.multiple_of(i * 448, 448), 448), :] = zeros

    for buffer in terms:
        buffer[...] = jnp.zeros_like(buffer)

    get_idx.wait()

    def fetch(r):
        return pltpu.make_async_copy(ops_in.at[idx[0, r, 120]], ops.at[r], ops_sem.at[r])

    @pl.loop(0, CLASSES)
    def _(r):
        fetch(r).start()

    eye = mask16(iota((128, 128), 0) == iota((128, 128), 1))
    get_par.wait()
    for j in range(SPAN):
        get_blocks[j].wait()
        for c in range(3):
            m = dot_nt(eye, blocks[j, c, 0:256, :])
            for q in range(2):
                win[pl.ds(j * 1024 + 2 * c + q, 128, stride=8), :] = m[:, 128 * q : 128 * q + 128]
        tails = jnp.concatenate(
            [blocks[j, c, 256:296, :] for c in range(3)] + [jnp.zeros((8, 128), bf16)], axis=0
        )
        win[pl.ds(j * 1024 + 6, 128, stride=8), :] = dot_nt(eye, tails)
        for r in range(7):
            win[pl.ds((LEAVES + j * 16) * 8 + r, 16, stride=8), :] = par[j, r].astype(f32)

    def at(which, k, s):
        return pl.ds(pl.multiple_of(idx[which, k, s], 8), 8)

    def gather(k, b, n):
        for s in range(n):
            gathered[b][s * 8 : s * 8 + 8, :] = win[at(0, k, s), :]

    def scatter(k, b, n):
        for s in range(n):
            acc[s % CHAINS][at(1, k, s), :] += terms[b][s * 8 : s * 8 + 8, :]

    def multiply(k, b, n):
        rows = [gathered[b][pl.ds(r, n, stride=8), :] for r in range(7)]
        tails = (rows[6], pltpu.roll(rows[6], 88, 1), pltpu.roll(rows[6], 48, 1))
        x = jnp.concatenate(
            [
                jnp.concatenate(
                    [
                        rows[2 * c].astype(bf16),
                        rows[2 * c + 1].astype(bf16),
                        tails[c].astype(bf16)[:, :40],
                    ],
                    axis=1,
                )
                for c in range(3)
            ],
            axis=0,
        )
        y = jnp.dot(x, ops[k], preferred_element_type=f32)
        pieces = []
        for c in range(3):
            part = y[c * n : (c + 1) * n]
            for q in range(2):
                terms[b][pl.ds(2 * c + q, n, stride=8), :] = part[:, 128 * q : 128 * q + 128]
            pieces.append(jnp.concatenate([part[:, 256:296], jnp.zeros((n, 88), f32)], axis=1))
        terms[b][pl.ds(6, n, stride=8), :] = (
            pieces[0] + pltpu.roll(pieces[1], 40, 1) + pltpu.roll(pieces[2], 80, 1)
        )

    start = 0
    for bucket in BUCKETS:
        n = 16 * bucket
        end = idx[0, 64, bucket]

        @pl.when(end > start)
        def _():
            gather(STEP * start, 0, n)

        @pl.loop(start, end)
        def _(i):
            first = STEP * i
            for u in range(STEP):
                fetch(first + u).wait()
            for u in range(STEP):
                k, now, other = first + u, u % 2, 1 - u % 2
                gather(k + 1 if u < STEP - 1 else jnp.minimum(k + 1, CLASSES - 1), other, n)
                multiply(k, now, n)
                scatter(k - 1 if u else jnp.maximum(k - 1, 0), other, n)

        start = end
    scatter(CLASSES - 1, 1, SLOTS)

    def merge(first, count):
        rows = pl.ds(first, count)
        win[rows, :] = functools.reduce(lambda p, q: p + q, [a[rows, :] for a in acc])

    puts = []
    for j in range(SPAN):
        leaf, parent = j * 1024, LEAVES * 8 + j * 128
        merge(leaf, 1024)
        merge(parent, 128)
        for r in range(7):
            rows = win[pl.ds(leaf + r, 128, stride=8), :].astype(bf16)
            result[j, r, 0:128, :] = dot_nt(eye, rows).astype(bf16)
            result[j, r, 128:144, :] = win[pl.ds(parent + r, 16, stride=8), :].astype(bf16)
        puts.append(pltpu.make_async_copy(result.at[j], out.at[j], sem.at[7 + j]))
        puts[j].start()
    for put in puts:
        put.wait()


def return_kernel(
    partial, side, behind, ahead, mine_near, mine_far, from_near, from_far, send, recv, local
):
    out, out_ok, in_ok = sides()
    first, rest = pl.ds(0, 4), pl.ds(4, 3)
    staged = [
        pltpu.make_async_copy(src, dst, local.at[n])
        for n, (src, dst) in enumerate(
            (
                (partial.at[2 + out, first], mine_near),
                (partial.at[2 - 2 * out, rest], mine_far),
            )
        )
    ]
    for copy in staged:
        copy.start()
    copy = functools.partial(remote, send=send, recv=recv)
    lend_far = copy(partial.at[2 - 2 * out, first], from_near, n=0, offset=-out)
    lend_near = copy(partial.at[2 + out, rest], from_far, n=1, offset=-out)
    to_side = copy(partial.at[2 - out], side, n=2, offset=-out)
    to_far = copy(partial.at[2 + 2 * out], behind, n=3, offset=2 * out)
    sum_near = copy(mine_near, ahead.at[first], n=4, offset=out)
    sum_far = copy(mine_far, ahead.at[rest], n=5, offset=-2 * out)
    greet()
    await_greetings()

    @pl.when(in_ok)
    def _():
        lend_far.start()

    @pl.when(out_ok)
    def _():
        lend_near.start()
        to_far.start()

    to_side.start()
    for c in staged:
        c.wait()

    def add(mine, theirs):
        mine[...] = (mine[...].astype(f32) + theirs[...].astype(f32)).astype(bf16)

    @pl.when(out_ok)
    def _():
        lend_far.wait_recv()
        add(mine_near, from_near)
        sum_near.start()

    @pl.when(in_ok)
    def _():
        lend_near.wait_recv()
        add(mine_far, from_far)
        sum_far.start()

    to_side.wait()

    @pl.when(out_ok)
    def _():
        lend_near.wait_send()
        to_far.wait_send()
        sum_near.wait()
        sum_far.wait_recv()

    @pl.when(in_ok)
    def _():
        lend_far.wait_send()
        to_far.wait_recv()
        sum_far.wait_send()


def sum_kernel(partial, side, behind, ahead, leaf, parent, got, leaf_sum, parent_sum, get, put):
    pieces = (pl.ds(6, 1), pl.ds(0, 2), pl.ds(2, 2), pl.ds(4, 2))
    gets = [
        [
            pltpu.make_async_copy(src.at[rows], got.at[n, rows], get.at[4 * p + n])
            for n, src in enumerate((partial.at[2], side, behind, ahead))
        ]
        for p, rows in enumerate(pieces)
    ]
    for piece in gets:
        for copy in piece:
            copy.start()
    _, out_ok, in_ok = sides()

    def total(r):
        s = got[0, r].astype(f32) + got[1, r].astype(f32)
        s = s + jnp.where(in_ok, got[2, r].astype(f32), 0.0)
        return s + jnp.where(out_ok, got[3, r].astype(f32), 0.0)

    for copy in gets[0]:
        copy.wait()
    tails = total(6)
    puts = []
    for c in range(3):
        for copy in gets[1 + c]:
            copy.wait()
        for q in range(2):
            s = total(2 * c + q)
            leaf_sum[c, 128 * q : 128 * q + 128, :] = s[0:128]
            parent_sum[c, :, 128 * q : 128 * q + 128] = s[128:144]
        leaf_sum[c, 256:296, :] = tails[40 * c : 40 * c + 40]
        shifted = tails[128:144] if c == 0 else pltpu.roll(tails[128:144], 128 - 40 * c, 1)
        parent_sum[c, :, 256:296] = shifted[:, :40]
        puts.append(pltpu.make_async_copy(leaf_sum.at[c], leaf.at[c], put.at[c]))
        puts[c].start()
    puts.append(pltpu.make_async_copy(parent_sum, parent, put.at[3]))
    puts[3].start()
    for copy in puts:
        copy.wait()


def on_device(multipole, m2m_ops, m2l_ops, lt, ls, pt, ps):
    mp = jnp.transpose(multipole, (1, 2, 0))
    pt, ps = jnp.transpose(pt[0]), jnp.transpose(ps[0])
    hbm = pl.BlockSpec(memory_space=pltpu.HBM)
    semaphores = pltpu.SemaphoreType.DMA
    rem, par, idx = pl.pallas_call(
        exchange_kernel,
        out_shape=(
            jax.ShapeDtypeStruct((SPAN, 3, P_SIZE, BOX_DEV), bf16),
            jax.ShapeDtypeStruct((SPAN, 7, PAR_DEV, 128), bf16),
            jax.ShapeDtypeStruct((2, 72, 128), jnp.int32),
        ),
        in_specs=[hbm] * 6,
        out_specs=(hbm, hbm, hbm),
        scratch_shapes=[
            pltpu.VMEM((3, P_SIZE, BOX_DEV), bf16),
            pltpu.VMEM((8, P_SIZE, P_SIZE), bf16),
            pltpu.VMEM((7, PAR_DEV, 128), bf16),
            pltpu.VMEM((CLASSES, SLOT), jnp.int32),
            pltpu.VMEM((CLASSES, SLOT), jnp.int32),
            pltpu.VMEM((PSLOT, CLASSES), jnp.int32),
            pltpu.VMEM((PSLOT, CLASSES), jnp.int32),
            pltpu.VMEM((CLASSES * 8, 128), f32),
            pltpu.VMEM((CLASSES, 128), f32),
            pltpu.VMEM((CLASSES * 8, 128), f32),
            pltpu.VMEM((2, 72, 128), jnp.int32),
            semaphores((6,)),
            semaphores((6,)),
            semaphores((6,)),
            semaphores((6,)),
            semaphores((8,)),
        ],
        compiler_params=pltpu.CompilerParams(
            collective_id=0, has_side_effects=True, vmem_limit_bytes=VMEM_BYTES
        ),
        name="exchange",
    )(mp, m2m_ops, lt[0], ls[0], pt, ps)
    partial = pl.pallas_call(
        translate_kernel,
        out_shape=jax.ShapeDtypeStruct((SPAN, 7, BOX_DEV + PAR_DEV, 128), bf16),
        in_specs=[hbm] * 5,
        out_specs=hbm,
        scratch_shapes=[
            pltpu.SMEM((2, 72, 128), jnp.int32),
            pltpu.VMEM((SPAN, 3, P_SIZE, BOX_DEV), bf16),
            pltpu.VMEM((SPAN, 7, PAR_DEV, 128), bf16),
            pltpu.VMEM((SPAN, 7, BOX_DEV + PAR_DEV, 128), bf16),
            pltpu.VMEM((ROWS * 8, 128), f32),
        ]
        + [pltpu.VMEM((SLOTS * 8, 128), f32)] * 4
        + [pltpu.VMEM((CLASSES, P_SIZE, P_SIZE), bf16), semaphores((CLASSES,)), semaphores((12,))]
        + [pltpu.VMEM((ACC_ROWS * 8, 128), f32)] * CHAINS,
        compiler_params=pltpu.CompilerParams(vmem_limit_bytes=VMEM_BYTES),
        name="translate",
    )(idx, mp, rem, par, m2l_ops)
    block = (7, BOX_DEV + PAR_DEV, 128)
    results = (
        jax.ShapeDtypeStruct((3, P_SIZE, BOX_DEV), f32),
        jax.ShapeDtypeStruct((3, PAR_DEV, P_SIZE), f32),
    )
    side, behind, ahead = pl.pallas_call(
        return_kernel,
        out_shape=(jax.ShapeDtypeStruct(block, bf16),) * 3,
        in_specs=[hbm],
        out_specs=(hbm,) * 3,
        scratch_shapes=[
            pltpu.VMEM((4,) + block[1:], bf16),
            pltpu.VMEM((3,) + block[1:], bf16),
            pltpu.VMEM((4,) + block[1:], bf16),
            pltpu.VMEM((3,) + block[1:], bf16),
            semaphores((6,)),
            semaphores((6,)),
            semaphores((2,)),
        ],
        compiler_params=pltpu.CompilerParams(
            collective_id=1, has_side_effects=True, vmem_limit_bytes=VMEM_BYTES
        ),
        name="return",
    )(partial)
    leaf, parent = pl.pallas_call(
        sum_kernel,
        out_shape=results,
        in_specs=[hbm] * 4,
        out_specs=(hbm, hbm),
        scratch_shapes=[
            pltpu.VMEM((4,) + block, bf16),
            pltpu.VMEM((3, P_SIZE, BOX_DEV), f32),
            pltpu.VMEM((3, PAR_DEV, P_SIZE), f32),
            semaphores((16,)),
            semaphores((4,)),
        ],
        compiler_params=pltpu.CompilerParams(vmem_limit_bytes=VMEM_BYTES),
        name="sums",
    )(partial, side, behind, ahead)
    return jnp.transpose(leaf, (2, 0, 1)), jnp.transpose(parent, (1, 0, 2))


def solution(mesh):
    boxes = P(("gx", "gy"), None, None)
    return jax.shard_map(
        on_device,
        mesh=mesh,
        in_specs=(boxes, P(), P(), boxes, boxes, boxes, boxes),
        out_specs=(boxes, boxes),
        check_vma=False,
    )
```

```python
import functools

import jax
import jax.numpy as jnp
from jax import lax
from jax.experimental import pallas as pl
from jax.experimental.pallas import tpu as pltpu
from jax.sharding import PartitionSpec as P

CLASSES = 64
SLOT = 80
PSLOT = 32
BUCKETS = (3, 4, 5, 6, 7)
STEP = 4
SLOTS = SLOT + PSLOT
P_SIZE = 296
BOX_DEV = 128
PAR_DEV = 16
SPAN = 5
LEAVES = SPAN * BOX_DEV
ROWS = LEAVES + SPAN * PAR_DEV
ACC_ROWS = ROWS + 8
CHAINS = 4
DEVICES = 128
VMEM_BYTES = 63 * 1024 * 1024
N_GY = 8
MESH = pl.DeviceIdType.MESH
f32 = jnp.float32
bf16 = jnp.bfloat16


def dot_nt(a, b):
    return lax.dot_general(a, b, (((1,), (1,)), ((), ())), preferred_element_type=f32)


def mask16(x):
    return x.astype(f32).astype(bf16)


def iota(shape, dim):
    return lax.broadcasted_iota(jnp.int32, shape, dim)


def here():
    return lax.axis_index("gx") * N_GY + lax.axis_index("gy")


def device_at(offset):
    index = lax.rem(here() + (offset + DEVICES), DEVICES)
    return (lax.div(index, N_GY), lax.rem(index, N_GY))


def sides():
    me = here()
    out = 2 * lax.rem(me, 2) - 1
    ahead, behind = me + 2 * out, me - 2 * out
    return out, (ahead >= 0) & (ahead < DEVICES), (behind >= 0) & (behind < DEVICES)


def entry_barrier():
    barrier = pltpu.get_barrier_semaphore()
    out, out_ok, in_ok = sides()

    def greet(offset):
        pl.semaphore_signal(barrier, inc=1, device_id=device_at(offset), device_id_type=MESH)

    greet(-out)

    @pl.when(out_ok)
    def _():
        greet(out)
        greet(2 * out)

    @pl.when(in_ok)
    def _():
        greet(-2 * out)

    pl.semaphore_wait(barrier, 1 + 2 * out_ok.astype(jnp.int32) + in_ok.astype(jnp.int32))


def remote(src, dst, send, recv, n, offset):
    return pltpu.make_async_remote_copy(
        src_ref=src,
        dst_ref=dst,
        send_sem=send.at[n],
        recv_sem=recv.at[n],
        device_id=device_at(offset),
        device_id_type=MESH,
    )


class Spread:
    def __init__(self, own, blocks, cut, send, recv):
        out, self.out_ok, self.in_ok = sides()
        first, rest = pl.ds(0, cut), pl.ds(cut, own.shape[0] - cut)
        copy = functools.partial(remote, send=send, recv=recv)
        self.sibling = copy(own, blocks.at[2 + out], n=0, offset=-out)
        self.behind = copy(own, blocks.at[2 + 2 * out], n=1, offset=-2 * out)
        self.near = copy(own.at[first], blocks.at[2 - out, first], n=2, offset=out)
        self.far = copy(own.at[rest], blocks.at[2 - 2 * out, rest], n=3, offset=2 * out)
        self.relay_near = copy(
            blocks.at[2 + out, first], blocks.at[2 + 2 * out, first], n=4, offset=-out
        )
        self.relay_far = copy(
            blocks.at[2 - 2 * out, rest], blocks.at[2 - out, rest], n=5, offset=-out
        )

    def start(self):
        @pl.when(self.out_ok)
        def _():
            self.near.start()
            self.far.start()

        @pl.when(self.in_ok)
        def _():
            self.behind.start()

        self.sibling.start()

    def relay(self):
        @pl.when(self.out_ok)
        def _():
            self.near.wait_recv()
            self.relay_near.start()

        @pl.when(self.in_ok)
        def _():
            self.far.wait_recv()
            self.relay_far.start()

    def finish(self):
        self.sibling.wait()

        @pl.when(self.out_ok)
        def _():
            self.near.wait_send()
            self.far.wait_send()
            self.behind.wait_recv()
            self.relay_near.wait_send()
            self.relay_far.wait_recv()

        @pl.when(self.in_ok)
        def _():
            self.behind.wait_send()
            self.relay_far.wait_send()
            self.relay_near.wait_recv()


def prepare_lists(ls, lt, ps, pt, leaf_base, par_base, values, place, packed, idx):
    eye = mask16(iota((64, 64), 0) == iota((64, 64), 1))

    def together(leaf, parent):
        low = jnp.concatenate(
            [jnp.zeros((80, 64), bf16), mask16(parent), jnp.zeros((16, 64), bf16)], axis=0
        )
        high = jnp.concatenate([leaf.astype(f32), jnp.zeros((64, 48), f32)], axis=1)
        return high + dot_nt(eye, low)

    leaf_live, par_live = ls[...] >= 0, ps[...] >= 0
    sl = jnp.where(leaf_live, ls[...] - leaf_base, 0)
    tl = jnp.where(leaf_live, lt[...] - leaf_base, 0)
    sp = jnp.where(par_live, ps[...] - par_base, 0)
    tp = jnp.where(par_live, pt[...] - par_base, 0)
    parts = [
        together(sl >> 3, sp >> 3),
        together(sl & 7, sp & 7),
        together(tl >> 3, tp >> 3),
        together(tl & 7, tp & 7),
        together(leaf_live, par_live),
    ]
    live = parts[4].astype(bf16)
    earlier = mask16(iota((128, 128), 0) < iota((128, 128), 1))
    before = jnp.dot(live, earlier, preferred_element_type=f32)
    place[...] = jnp.where(parts[4] > 0.5, before, 200.0)
    values[...] = jnp.zeros_like(values)
    for q, part in enumerate(parts):
        values[pl.ds(q, 64, stride=8), :] = part
    wanted = iota((128, 128), 0).astype(f32)

    @pl.loop(0, CLASSES, unroll=16)
    def _(k):
        hit = mask16(wanted == place[pl.ds(k, 1), :])
        rows = pl.ds(pl.multiple_of(k * 8, 8), 8)
        packed[rows, :] = dot_nt(values[rows, :].astype(bf16), hit)

    ones = jnp.ones((128, 128), bf16)
    count = jnp.dot(live, ones, preferred_element_type=f32)
    count_row = dot_nt(ones[0:16], live)[0:1, :]
    row, column = iota((64, 64), 0), iota((64, 64), 1)
    count_column = count[:, 0:64]
    ahead = mask16(
        (count_row < count_column) | ((count_row == count_column) & (column < row))
    )
    rank = dot_nt(ones[0:16, 0:64], ahead)[0:1, :]
    perm = mask16(rank == row.astype(f32))

    def sort(v):
        return jnp.dot(perm, v.astype(bf16), preferred_element_type=f32)

    s_high, s_low, t_high, t_low, used = (
        sort(packed[pl.ds(q, 64, stride=8), :]) for q in range(5)
    )
    order = sort(iota((64, 128), 0).astype(f32))
    lane = iota((64, 128), 1)
    source = (s_high * 8 + s_low) * 8
    target = jnp.where(used > 0.5, t_high * 8 + t_low, float(ROWS)) * 8
    idx[0, 0:64, :] = jnp.where(lane == 120, order, source).astype(jnp.int32)
    idx[1, 0:64, :] = target.astype(jnp.int32)
    fits = mask16(count <= (16 * lane).astype(f32))
    groups = jnp.dot(ones[0:16, 0:64], fits, preferred_element_type=f32)[0:8]
    idx[0, 64:72, :] = groups.astype(jnp.int32) // STEP
    idx[1, 64:72, :] = jnp.zeros((8, 128), jnp.int32)


def exchange_kernel(
    mp, m2m, lt_in, ls_in, pt_in, ps_in, rem, par, idx_out,
    own, ops, par_own, lt, ls, pt, ps, values, place, packed, idx,
    send, recv, psend, precv, local,
):
    staged = [
        pltpu.make_async_copy(src, dst, local.at[n])
        for n, (src, dst) in enumerate(
            ((mp, own), (m2m, ops), (lt_in, lt), (ls_in, ls), (pt_in, pt), (ps_in, ps))
        )
    ]
    for copy in staged:
        copy.start()
    entry_barrier()
    leaves = Spread(mp, rem, 2, send, recv)
    leaves.start()
    for copy in staged:
        copy.wait()

    row = iota((128, 128), 0)
    select = mask16(iota((128, 128), 1) == 8 * (row & 15) + (row >> 4))
    by_octant = [dot_nt(select, own[c]).astype(bf16) for c in range(3)]
    total = jnp.zeros((48, P_SIZE), f32)
    for o in range(8):
        rows = jnp.concatenate([by_octant[c][16 * o : 16 * o + 16] for c in range(3)], axis=0)
        total = total + jnp.dot(rows, ops[o], preferred_element_type=f32)
    pieces = []
    for c in range(3):
        part = total[16 * c : 16 * c + 16]
        for q in range(2):
            par_own[2 * c + q] = part[:, 128 * q : 128 * q + 128].astype(bf16)
        pieces.append(jnp.concatenate([part[:, 256:296], jnp.zeros((16, 88), f32)], axis=1))
    tails = pieces[0] + pltpu.roll(pieces[1], 40, 1) + pltpu.roll(pieces[2], 80, 1)
    par_own[6] = tails.astype(bf16)
    keep = pltpu.make_async_copy(par_own, par.at[2], local.at[6])
    keep.start()
    out, out_ok, in_ok = sides()
    to_side, to_near, to_far, to_behind = (
        remote(par_own, par.at[2 - offset], psend, precv, n, offset)
        for n, offset in enumerate((-out, out, 2 * out, -2 * out))
    )
    to_side.start()

    @pl.when(out_ok)
    def _():
        to_near.start()
        to_far.start()

    @pl.when(in_ok)
    def _():
        to_behind.start()

    leaf_base = (here() - 2) * BOX_DEV
    par_base = (here() - 2) * PAR_DEV - LEAVES
    prepare_lists(ls, lt, ps, pt, leaf_base, par_base, values, place, packed, idx)
    put = pltpu.make_async_copy(idx, idx_out, local.at[7])
    put.start()

    leaves.relay()
    keep.wait()
    put.wait()
    leaves.finish()
    to_side.wait()

    @pl.when(out_ok)
    def _():
        to_near.wait()
        to_far.wait_send()
        to_behind.wait_recv()

    @pl.when(in_ok)
    def _():
        to_behind.wait_send()
        to_far.wait_recv()


def translate_kernel(
    idx_in, mp, rem, par_in, ops_in, out,
    idx, blocks, par, result, win, g0, g1, o0, o1, ops, ops_sem, sem, *acc,
):
    gathered, terms = (g0, g1), (o0, o1)
    get_idx = pltpu.make_async_copy(idx_in, idx, sem.at[0])
    get_idx.start()
    get_blocks = []
    for j in range(SPAN):
        src = mp if j == 2 else rem.at[j]
        get_blocks.append(pltpu.make_async_copy(src, blocks.at[j], sem.at[1 + j]))
        get_blocks[j].start()
    get_par = pltpu.make_async_copy(par_in, par, sem.at[6])
    get_par.start()

    zeros = jnp.zeros((448, 128), f32)
    for a in acc:

        @pl.loop(0, ACC_ROWS * 8 // 448)
        def _(i):
            a[pl.ds(pl.multiple_of(i * 448, 448), 448), :] = zeros

    for buffer in terms:
        buffer[...] = jnp.zeros_like(buffer)

    get_idx.wait()

    def fetch(r):
        return pltpu.make_async_copy(ops_in.at[idx[0, r, 120]], ops.at[r], ops_sem.at[r])

    @pl.loop(0, CLASSES)
    def _(r):
        fetch(r).start()

    eye = mask16(iota((128, 128), 0) == iota((128, 128), 1))
    get_par.wait()
    for j in range(SPAN):
        get_blocks[j].wait()
        for c in range(3):
            m = dot_nt(eye, blocks[j, c, 0:256, :])
            for q in range(2):
                win[pl.ds(j * 1024 + 2 * c + q, 128, stride=8), :] = m[:, 128 * q : 128 * q + 128]
        tails = jnp.concatenate(
            [blocks[j, c, 256:296, :] for c in range(3)] + [jnp.zeros((8, 128), bf16)], axis=0
        )
        win[pl.ds(j * 1024 + 6, 128, stride=8), :] = dot_nt(eye, tails)
        for r in range(7):
            win[pl.ds((LEAVES + j * 16) * 8 + r, 16, stride=8), :] = par[j, r].astype(f32)

    def at(which, k, s):
        return pl.ds(pl.multiple_of(idx[which, k, s], 8), 8)

    def gather(k, b, n):
        for s in range(n):
            gathered[b][s * 8 : s * 8 + 8, :] = win[at(0, k, s), :]

    def scatter(k, b, n):
        for s in range(n):
            acc[s % CHAINS][at(1, k, s), :] += terms[b][s * 8 : s * 8 + 8, :]

    def multiply(k, b, n):
        rows = [gathered[b][pl.ds(r, n, stride=8), :] for r in range(7)]
        tails = (rows[6], pltpu.roll(rows[6], 88, 1), pltpu.roll(rows[6], 48, 1))
        x = jnp.concatenate(
            [
                jnp.concatenate(
                    [
                        rows[2 * c].astype(bf16),
                        rows[2 * c + 1].astype(bf16),
                        tails[c].astype(bf16)[:, :40],
                    ],
                    axis=1,
                )
                for c in range(3)
            ],
            axis=0,
        )
        y = jnp.dot(x, ops[k], preferred_element_type=f32)
        pieces = []
        for c in range(3):
            part = y[c * n : (c + 1) * n]
            for q in range(2):
                terms[b][pl.ds(2 * c + q, n, stride=8), :] = part[:, 128 * q : 128 * q + 128]
            pieces.append(jnp.concatenate([part[:, 256:296], jnp.zeros((n, 88), f32)], axis=1))
        terms[b][pl.ds(6, n, stride=8), :] = (
            pieces[0] + pltpu.roll(pieces[1], 40, 1) + pltpu.roll(pieces[2], 80, 1)
        )

    start = 0
    for bucket in BUCKETS:
        n = 16 * bucket
        end = idx[0, 64, bucket]

        @pl.when(end > start)
        def _():
            gather(STEP * start, 0, n)

        @pl.loop(start, end)
        def _(i):
            first = STEP * i
            for u in range(STEP):
                fetch(first + u).wait()
            for u in range(STEP):
                k, now, other = first + u, u % 2, 1 - u % 2
                gather(k + 1 if u < STEP - 1 else jnp.minimum(k + 1, CLASSES - 1), other, n)
                multiply(k, now, n)
                scatter(k - 1 if u else jnp.maximum(k - 1, 0), other, n)

        start = end
    scatter(CLASSES - 1, 1, SLOTS)

    def merge(first, count):
        rows = pl.ds(first, count)
        win[rows, :] = functools.reduce(lambda p, q: p + q, [a[rows, :] for a in acc])

    puts = []
    for j in range(SPAN):
        leaf, parent = j * 1024, LEAVES * 8 + j * 128
        merge(leaf, 1024)
        merge(parent, 128)
        for r in range(7):
            rows = win[pl.ds(leaf + r, 128, stride=8), :].astype(bf16)
            result[j, r, 0:128, :] = dot_nt(eye, rows).astype(bf16)
            result[j, r, 128:144, :] = win[pl.ds(parent + r, 16, stride=8), :].astype(bf16)
        puts.append(pltpu.make_async_copy(result.at[j], out.at[j], sem.at[7 + j]))
        puts[j].start()
    for put in puts:
        put.wait()


def return_kernel(
    partial, side, behind, ahead, mine_near, mine_far, from_near, from_far, send, recv, local
):
    out, out_ok, in_ok = sides()
    first, rest = pl.ds(0, 4), pl.ds(4, 3)
    staged = [
        pltpu.make_async_copy(src, dst, local.at[n])
        for n, (src, dst) in enumerate(
            (
                (partial.at[2 + out, first], mine_near),
                (partial.at[2 - 2 * out, rest], mine_far),
            )
        )
    ]
    for copy in staged:
        copy.start()
    copy = functools.partial(remote, send=send, recv=recv)
    lend_far = copy(partial.at[2 - 2 * out, first], from_near, n=0, offset=-out)
    lend_near = copy(partial.at[2 + out, rest], from_far, n=1, offset=-out)
    to_side = copy(partial.at[2 - out], side, n=2, offset=-out)
    to_far = copy(partial.at[2 + 2 * out], behind, n=3, offset=2 * out)
    sum_near = copy(mine_near, ahead.at[first], n=4, offset=out)
    sum_far = copy(mine_far, ahead.at[rest], n=5, offset=-2 * out)
    entry_barrier()

    @pl.when(in_ok)
    def _():
        lend_far.start()

    @pl.when(out_ok)
    def _():
        lend_near.start()
        to_far.start()

    to_side.start()
    for c in staged:
        c.wait()

    def add(mine, theirs):
        mine[...] = (mine[...].astype(f32) + theirs[...].astype(f32)).astype(bf16)

    @pl.when(out_ok)
    def _():
        lend_far.wait_recv()
        add(mine_near, from_near)
        sum_near.start()

    @pl.when(in_ok)
    def _():
        lend_near.wait_recv()
        add(mine_far, from_far)
        sum_far.start()

    to_side.wait()

    @pl.when(out_ok)
    def _():
        lend_near.wait_send()
        to_far.wait_send()
        sum_near.wait()
        sum_far.wait_recv()

    @pl.when(in_ok)
    def _():
        lend_far.wait_send()
        to_far.wait_recv()
        sum_far.wait_send()


def sum_kernel(partial, side, behind, ahead, leaf, parent, got, leaf_sum, parent_sum, get, put):
    pieces = (pl.ds(6, 1), pl.ds(0, 2), pl.ds(2, 2), pl.ds(4, 2))
    gets = [
        [
            pltpu.make_async_copy(src.at[rows], got.at[n, rows], get.at[4 * p + n])
            for n, src in enumerate((partial.at[2], side, behind, ahead))
        ]
        for p, rows in enumerate(pieces)
    ]
    for piece in gets:
        for copy in piece:
            copy.start()
    _, out_ok, in_ok = sides()

    def total(r):
        s = got[0, r].astype(f32) + got[1, r].astype(f32)
        s = s + jnp.where(in_ok, got[2, r].astype(f32), 0.0)
        return s + jnp.where(out_ok, got[3, r].astype(f32), 0.0)

    for copy in gets[0]:
        copy.wait()
    tails = total(6)
    puts = []
    for c in range(3):
        for copy in gets[1 + c]:
            copy.wait()
        for q in range(2):
            s = total(2 * c + q)
            leaf_sum[c, 128 * q : 128 * q + 128, :] = s[0:128]
            parent_sum[c, :, 128 * q : 128 * q + 128] = s[128:144]
        leaf_sum[c, 256:296, :] = tails[40 * c : 40 * c + 40]
        shifted = tails[128:144] if c == 0 else pltpu.roll(tails[128:144], 128 - 40 * c, 1)
        parent_sum[c, :, 256:296] = shifted[:, :40]
        puts.append(pltpu.make_async_copy(leaf_sum.at[c], leaf.at[c], put.at[c]))
        puts[c].start()
    puts.append(pltpu.make_async_copy(parent_sum, parent, put.at[3]))
    puts[3].start()
    for copy in puts:
        copy.wait()


def on_device(multipole, m2m_ops, m2l_ops, lt, ls, pt, ps):
    mp = jnp.transpose(multipole, (1, 2, 0))
    pt, ps = jnp.transpose(pt[0]), jnp.transpose(ps[0])
    hbm = pl.BlockSpec(memory_space=pltpu.HBM)
    semaphores = pltpu.SemaphoreType.DMA
    rem, par, idx = pl.pallas_call(
        exchange_kernel,
        out_shape=(
            jax.ShapeDtypeStruct((SPAN, 3, P_SIZE, BOX_DEV), bf16),
            jax.ShapeDtypeStruct((SPAN, 7, PAR_DEV, 128), bf16),
            jax.ShapeDtypeStruct((2, 72, 128), jnp.int32),
        ),
        in_specs=[hbm] * 6,
        out_specs=(hbm, hbm, hbm),
        scratch_shapes=[
            pltpu.VMEM((3, P_SIZE, BOX_DEV), bf16),
            pltpu.VMEM((8, P_SIZE, P_SIZE), bf16),
            pltpu.VMEM((7, PAR_DEV, 128), bf16),
            pltpu.VMEM((CLASSES, SLOT), jnp.int32),
            pltpu.VMEM((CLASSES, SLOT), jnp.int32),
            pltpu.VMEM((PSLOT, CLASSES), jnp.int32),
            pltpu.VMEM((PSLOT, CLASSES), jnp.int32),
            pltpu.VMEM((CLASSES * 8, 128), f32),
            pltpu.VMEM((CLASSES, 128), f32),
            pltpu.VMEM((CLASSES * 8, 128), f32),
            pltpu.VMEM((2, 72, 128), jnp.int32),
            semaphores((6,)),
            semaphores((6,)),
            semaphores((4,)),
            semaphores((4,)),
            semaphores((8,)),
        ],
        compiler_params=pltpu.CompilerParams(
            collective_id=0, has_side_effects=True, vmem_limit_bytes=VMEM_BYTES
        ),
        name="exchange",
    )(mp, m2m_ops, lt[0], ls[0], pt, ps)
    partial = pl.pallas_call(
        translate_kernel,
        out_shape=jax.ShapeDtypeStruct((SPAN, 7, BOX_DEV + PAR_DEV, 128), bf16),
        in_specs=[hbm] * 5,
        out_specs=hbm,
        scratch_shapes=[
            pltpu.SMEM((2, 72, 128), jnp.int32),
            pltpu.VMEM((SPAN, 3, P_SIZE, BOX_DEV), bf16),
            pltpu.VMEM((SPAN, 7, PAR_DEV, 128), bf16),
            pltpu.VMEM((SPAN, 7, BOX_DEV + PAR_DEV, 128), bf16),
            pltpu.VMEM((ROWS * 8, 128), f32),
        ]
        + [pltpu.VMEM((SLOTS * 8, 128), f32)] * 4
        + [pltpu.VMEM((CLASSES, P_SIZE, P_SIZE), bf16), semaphores((CLASSES,)), semaphores((12,))]
        + [pltpu.VMEM((ACC_ROWS * 8, 128), f32)] * CHAINS,
        compiler_params=pltpu.CompilerParams(vmem_limit_bytes=VMEM_BYTES),
        name="translate",
    )(idx, mp, rem, par, m2l_ops)
    block = (7, BOX_DEV + PAR_DEV, 128)
    results = (
        jax.ShapeDtypeStruct((3, P_SIZE, BOX_DEV), f32),
        jax.ShapeDtypeStruct((3, PAR_DEV, P_SIZE), f32),
    )
    side, behind, ahead = pl.pallas_call(
        return_kernel,
        out_shape=(jax.ShapeDtypeStruct(block, bf16),) * 3,
        in_specs=[hbm],
        out_specs=(hbm,) * 3,
        scratch_shapes=[
            pltpu.VMEM((4,) + block[1:], bf16),
            pltpu.VMEM((3,) + block[1:], bf16),
            pltpu.VMEM((4,) + block[1:], bf16),
            pltpu.VMEM((3,) + block[1:], bf16),
            semaphores((6,)),
            semaphores((6,)),
            semaphores((2,)),
        ],
        compiler_params=pltpu.CompilerParams(
            collective_id=1, has_side_effects=True, vmem_limit_bytes=VMEM_BYTES
        ),
        name="return",
    )(partial)
    leaf, parent = pl.pallas_call(
        sum_kernel,
        out_shape=results,
        in_specs=[hbm] * 4,
        out_specs=(hbm, hbm),
        scratch_shapes=[
            pltpu.VMEM((4,) + block, bf16),
            pltpu.VMEM((3, P_SIZE, BOX_DEV), f32),
            pltpu.VMEM((3, PAR_DEV, P_SIZE), f32),
            semaphores((16,)),
            semaphores((4,)),
        ],
        compiler_params=pltpu.CompilerParams(vmem_limit_bytes=VMEM_BYTES),
        name="sums",
    )(partial, side, behind, ahead)
    return jnp.transpose(leaf, (2, 0, 1)), jnp.transpose(parent, (1, 0, 2))


def solution(mesh):
    boxes = P(("gx", "gy"), None, None)
    return jax.shard_map(
        on_device,
        mesh=mesh,
        in_specs=(boxes, P(), P(), boxes, boxes, boxes, boxes),
        out_specs=(boxes, boxes),
        check_vma=False,
    )
```

```python
import functools

import jax
import jax.numpy as jnp
from jax import lax
from jax.experimental import pallas as pl
from jax.experimental.pallas import tpu as pltpu
from jax.sharding import PartitionSpec as P

CLASSES = 64
SLOT = 80
PSLOT = 32
BUCKETS = (3, 4, 5, 6, 7)
STEP = 4
SLOTS = SLOT + PSLOT
P_SIZE = 296
BOX_DEV = 128
PAR_DEV = 16
SPAN = 5
LEAVES = SPAN * BOX_DEV
ROWS = LEAVES + SPAN * PAR_DEV
ACC_ROWS = ROWS + 8
CHAINS = 4
DEVICES = 128
VMEM_BYTES = 63 * 1024 * 1024
N_GY = 8
MESH = pl.DeviceIdType.MESH
f32 = jnp.float32
bf16 = jnp.bfloat16


def dot_nt(a, b):
    return lax.dot_general(a, b, (((1,), (1,)), ((), ())), preferred_element_type=f32)


def mask16(x):
    return x.astype(f32).astype(bf16)


def iota(shape, dim):
    return lax.broadcasted_iota(jnp.int32, shape, dim)


def here():
    return lax.axis_index("gx") * N_GY + lax.axis_index("gy")


def device_at(offset):
    index = lax.rem(here() + (offset + DEVICES), DEVICES)
    return (lax.div(index, N_GY), lax.rem(index, N_GY))


def sides():
    me = here()
    out = 2 * lax.rem(me, 2) - 1
    ahead, behind = me + 2 * out, me - 2 * out
    return out, (ahead >= 0) & (ahead < DEVICES), (behind >= 0) & (behind < DEVICES)


def entry_barrier():
    barrier = pltpu.get_barrier_semaphore()
    out, out_ok, in_ok = sides()

    def greet(offset):
        pl.semaphore_signal(barrier, inc=1, device_id=device_at(offset), device_id_type=MESH)

    greet(-out)

    @pl.when(out_ok)
    def _():
        greet(out)
        greet(2 * out)

    @pl.when(in_ok)
    def _():
        greet(-2 * out)

    pl.semaphore_wait(barrier, 1 + 2 * out_ok.astype(jnp.int32) + in_ok.astype(jnp.int32))


def remote(src, dst, send, recv, n, offset):
    return pltpu.make_async_remote_copy(
        src_ref=src,
        dst_ref=dst,
        send_sem=send.at[n],
        recv_sem=recv.at[n],
        device_id=device_at(offset),
        device_id_type=MESH,
    )


class Spread:
    def __init__(self, own, blocks, cut, send, recv):
        out, self.out_ok, self.in_ok = sides()
        first, rest = pl.ds(0, cut), pl.ds(cut, own.shape[0] - cut)
        copy = functools.partial(remote, send=send, recv=recv)
        self.sibling = copy(own, blocks.at[2 + out], n=0, offset=-out)
        self.behind = copy(own, blocks.at[2 + 2 * out], n=1, offset=-2 * out)
        self.near = copy(own.at[first], blocks.at[2 - out, first], n=2, offset=out)
        self.far = copy(own.at[rest], blocks.at[2 - 2 * out, rest], n=3, offset=2 * out)
        self.relay_near = copy(
            blocks.at[2 + out, first], blocks.at[2 + 2 * out, first], n=4, offset=-out
        )
        self.relay_far = copy(
            blocks.at[2 - 2 * out, rest], blocks.at[2 - out, rest], n=5, offset=-out
        )

    def start(self):
        @pl.when(self.out_ok)
        def _():
            self.near.start()
            self.far.start()

        @pl.when(self.in_ok)
        def _():
            self.behind.start()

        self.sibling.start()

    def relay(self):
        @pl.when(self.out_ok)
        def _():
            self.near.wait_recv()
            self.relay_near.start()

        @pl.when(self.in_ok)
        def _():
            self.far.wait_recv()
            self.relay_far.start()

    def finish(self):
        self.sibling.wait()

        @pl.when(self.out_ok)
        def _():
            self.near.wait_send()
            self.far.wait_send()
            self.behind.wait_recv()
            self.relay_near.wait_send()
            self.relay_far.wait_recv()

        @pl.when(self.in_ok)
        def _():
            self.behind.wait_send()
            self.relay_far.wait_send()
            self.relay_near.wait_recv()


def prepare_lists(ls, lt, ps, pt, leaf_base, par_base, values, place, packed, idx):
    eye = mask16(iota((64, 64), 0) == iota((64, 64), 1))

    def together(leaf, parent):
        low = jnp.concatenate(
            [jnp.zeros((80, 64), bf16), mask16(parent), jnp.zeros((16, 64), bf16)], axis=0
        )
        high = jnp.concatenate([leaf.astype(f32), jnp.zeros((64, 48), f32)], axis=1)
        return high + dot_nt(eye, low)

    leaf_live, par_live = ls[...] >= 0, ps[...] >= 0
    sl = jnp.where(leaf_live, ls[...] - leaf_base, 0)
    tl = jnp.where(leaf_live, lt[...] - leaf_base, 0)
    sp = jnp.where(par_live, ps[...] - par_base, 0)
    tp = jnp.where(par_live, pt[...] - par_base, 0)
    parts = [
        together(sl >> 3, sp >> 3),
        together(sl & 7, sp & 7),
        together(tl >> 3, tp >> 3),
        together(tl & 7, tp & 7),
        together(leaf_live, par_live),
    ]
    live = parts[4].astype(bf16)
    earlier = mask16(iota((128, 128), 0) < iota((128, 128), 1))
    before = jnp.dot(live, earlier, preferred_element_type=f32)
    place[...] = jnp.where(parts[4] > 0.5, before, 200.0)
    values[...] = jnp.zeros_like(values)
    for q, part in enumerate(parts):
        values[pl.ds(q, 64, stride=8), :] = part
    wanted = iota((128, 128), 0).astype(f32)

    @pl.loop(0, CLASSES, unroll=16)
    def _(k):
        hit = mask16(wanted == place[pl.ds(k, 1), :])
        rows = pl.ds(pl.multiple_of(k * 8, 8), 8)
        packed[rows, :] = dot_nt(values[rows, :].astype(bf16), hit)

    ones = jnp.ones((128, 128), bf16)
    count = jnp.dot(live, ones, preferred_element_type=f32)
    count_row = dot_nt(ones[0:16], live)[0:1, :]
    row, column = iota((64, 64), 0), iota((64, 64), 1)
    count_column = count[:, 0:64]
    ahead = mask16(
        (count_row < count_column) | ((count_row == count_column) & (column < row))
    )
    rank = dot_nt(ones[0:16, 0:64], ahead)[0:1, :]
    perm = mask16(rank == row.astype(f32))

    def sort(v):
        return jnp.dot(perm, v.astype(bf16), preferred_element_type=f32)

    s_high, s_low, t_high, t_low, used = (
        sort(packed[pl.ds(q, 64, stride=8), :]) for q in range(5)
    )
    order = sort(iota((64, 128), 0).astype(f32))
    lane = iota((64, 128), 1)
    source = (s_high * 8 + s_low) * 8
    target = jnp.where(used > 0.5, t_high * 8 + t_low, float(ROWS)) * 8
    idx[0, 0:64, :] = jnp.where(lane == 120, order, source).astype(jnp.int32)
    idx[1, 0:64, :] = target.astype(jnp.int32)
    fits = mask16(count <= (16 * lane).astype(f32))
    groups = jnp.dot(ones[0:16, 0:64], fits, preferred_element_type=f32)[0:8]
    idx[0, 64:72, :] = groups.astype(jnp.int32) // STEP
    idx[1, 64:72, :] = jnp.zeros((8, 128), jnp.int32)


def exchange_kernel(
    mp, m2m, lt_in, ls_in, pt_in, ps_in, rem, par, idx_out,
    own, ops, par_own, lt, ls, pt, ps, values, place, packed, idx,
    send, recv, psend, precv, local,
):
    staged = [
        pltpu.make_async_copy(src, dst, local.at[n])
        for n, (src, dst) in enumerate(
            ((mp, own), (m2m, ops), (lt_in, lt), (ls_in, ls), (pt_in, pt), (ps_in, ps))
        )
    ]
    for copy in staged:
        copy.start()
    entry_barrier()
    leaves = Spread(mp, rem, 2, send, recv)
    leaves.start()
    for copy in staged:
        copy.wait()

    row = iota((128, 128), 0)
    select = mask16(iota((128, 128), 1) == 8 * (row & 15) + (row >> 4))
    by_octant = [dot_nt(select, own[c]).astype(bf16) for c in range(3)]
    total = jnp.zeros((48, P_SIZE), f32)
    for o in range(8):
        rows = jnp.concatenate([by_octant[c][16 * o : 16 * o + 16] for c in range(3)], axis=0)
        total = total + jnp.dot(rows, ops[o], preferred_element_type=f32)
    pieces = []
    for c in range(3):
        part = total[16 * c : 16 * c + 16]
        for q in range(2):
            par_own[2 * c + q] = part[:, 128 * q : 128 * q + 128].astype(bf16)
        pieces.append(jnp.concatenate([part[:, 256:296], jnp.zeros((16, 88), f32)], axis=1))
    tails = pieces[0] + pltpu.roll(pieces[1], 40, 1) + pltpu.roll(pieces[2], 80, 1)
    par_own[6] = tails.astype(bf16)
    keep = pltpu.make_async_copy(par_own, par.at[2], local.at[6])
    keep.start()
    out, out_ok, in_ok = sides()
    to_side, to_near, to_far, to_behind = (
        remote(par_own, par.at[2 - offset], psend, precv, n, offset)
        for n, offset in enumerate((-out, out, 2 * out, -2 * out))
    )
    to_side.start()

    @pl.when(out_ok)
    def _():
        to_near.start()
        to_far.start()

    @pl.when(in_ok)
    def _():
        to_behind.start()

    leaf_base = (here() - 2) * BOX_DEV
    par_base = (here() - 2) * PAR_DEV - LEAVES
    prepare_lists(ls, lt, ps, pt, leaf_base, par_base, values, place, packed, idx)
    put = pltpu.make_async_copy(idx, idx_out, local.at[7])
    put.start()

    leaves.relay()
    keep.wait()
    put.wait()
    leaves.finish()
    to_side.wait()

    @pl.when(out_ok)
    def _():
        to_near.wait()
        to_far.wait_send()
        to_behind.wait_recv()

    @pl.when(in_ok)
    def _():
        to_behind.wait_send()
        to_far.wait_recv()


def translate_kernel(
    idx_in, mp, rem, par_in, ops_in, out,
    idx, blocks, par, result, win, g0, g1, o0, o1, ops, ops_sem, sem, *acc,
):
    gathered, terms = (g0, g1), (o0, o1)
    get_idx = pltpu.make_async_copy(idx_in, idx, sem.at[0])
    get_idx.start()
    get_blocks = []
    for j in range(SPAN):
        src = mp if j == 2 else rem.at[j]
        get_blocks.append(pltpu.make_async_copy(src, blocks.at[j], sem.at[1 + j]))
        get_blocks[j].start()
    get_par = pltpu.make_async_copy(par_in, par, sem.at[6])
    get_par.start()

    zeros = jnp.zeros((448, 128), f32)
    for a in acc:

        @pl.loop(0, ACC_ROWS * 8 // 448)
        def _(i):
            a[pl.ds(pl.multiple_of(i * 448, 448), 448), :] = zeros

    for buffer in terms:
        buffer[...] = jnp.zeros_like(buffer)

    get_idx.wait()

    def fetch(r):
        return pltpu.make_async_copy(ops_in.at[idx[0, r, 120]], ops.at[r], ops_sem.at[r])

    @pl.loop(0, CLASSES)
    def _(r):
        fetch(r).start()

    eye = mask16(iota((128, 128), 0) == iota((128, 128), 1))
    get_par.wait()
    for j in range(SPAN):
        get_blocks[j].wait()
        for c in range(3):
            m = dot_nt(eye, blocks[j, c, 0:256, :])
            for q in range(2):
                win[pl.ds(j * 1024 + 2 * c + q, 128, stride=8), :] = m[:, 128 * q : 128 * q + 128]
        tails = jnp.concatenate(
            [blocks[j, c, 256:296, :] for c in range(3)] + [jnp.zeros((8, 128), bf16)], axis=0
        )
        win[pl.ds(j * 1024 + 6, 128, stride=8), :] = dot_nt(eye, tails)
        for r in range(7):
            win[pl.ds((LEAVES + j * 16) * 8 + r, 16, stride=8), :] = par[j, r].astype(f32)

    def at(which, k, s):
        return pl.ds(pl.multiple_of(idx[which, k, s], 8), 8)

    def gather(k, b, n):
        for s in range(n):
            gathered[b][s * 8 : s * 8 + 8, :] = win[at(0, k, s), :]

    def scatter(k, b, n):
        for s in range(n):
            acc[s % CHAINS][at(1, k, s), :] += terms[b][s * 8 : s * 8 + 8, :]

    def multiply(k, b, n):
        rows = [gathered[b][pl.ds(r, n, stride=8), :] for r in range(7)]
        tails = (rows[6], pltpu.roll(rows[6], 88, 1), pltpu.roll(rows[6], 48, 1))
        x = jnp.concatenate(
            [
                jnp.concatenate(
                    [
                        rows[2 * c].astype(bf16),
                        rows[2 * c + 1].astype(bf16),
                        tails[c].astype(bf16)[:, :40],
                    ],
                    axis=1,
                )
                for c in range(3)
            ],
            axis=0,
        )
        y = jnp.dot(x, ops[k], preferred_element_type=f32)
        pieces = []
        for c in range(3):
            part = y[c * n : (c + 1) * n]
            for q in range(2):
                terms[b][pl.ds(2 * c + q, n, stride=8), :] = part[:, 128 * q : 128 * q + 128]
            pieces.append(jnp.concatenate([part[:, 256:296], jnp.zeros((n, 88), f32)], axis=1))
        terms[b][pl.ds(6, n, stride=8), :] = (
            pieces[0] + pltpu.roll(pieces[1], 40, 1) + pltpu.roll(pieces[2], 80, 1)
        )

    start = 0
    for bucket in BUCKETS:
        n = 16 * bucket
        end = idx[0, 64, bucket]

        @pl.when(end > start)
        def _():
            gather(STEP * start, 0, n)

        @pl.loop(start, end)
        def _(i):
            first = STEP * i
            for u in range(STEP):
                fetch(first + u).wait()
            for u in range(STEP):
                k, now, other = first + u, u % 2, 1 - u % 2
                gather(k + 1 if u < STEP - 1 else jnp.minimum(k + 1, CLASSES - 1), other, n)
                multiply(k, now, n)
                scatter(k - 1 if u else jnp.maximum(k - 1, 0), other, n)

        start = end
    scatter(CLASSES - 1, 1, SLOTS)

    def merge(first, count):
        rows = pl.ds(first, count)
        win[rows, :] = functools.reduce(lambda p, q: p + q, [a[rows, :] for a in acc])

    puts = []
    for j in range(SPAN):
        leaf, parent = j * 1024, LEAVES * 8 + j * 128
        merge(leaf, 1024)
        merge(parent, 128)
        for r in range(7):
            rows = win[pl.ds(leaf + r, 128, stride=8), :].astype(bf16)
            result[j, r, 0:128, :] = dot_nt(eye, rows).astype(bf16)
            result[j, r, 128:144, :] = win[pl.ds(parent + r, 16, stride=8), :].astype(bf16)
        puts.append(pltpu.make_async_copy(result.at[j], out.at[j], sem.at[7 + j]))
        puts[j].start()
    for put in puts:
        put.wait()


def return_kernel(
    partial, side, behind, ahead, mine_near, mine_far, from_near, from_far, send, recv, local
):
    out, out_ok, in_ok = sides()
    first, rest = pl.ds(0, 4), pl.ds(4, 3)
    staged = [
        pltpu.make_async_copy(src, dst, local.at[n])
        for n, (src, dst) in enumerate(
            (
                (partial.at[2 + out, first], mine_near),
                (partial.at[2 - 2 * out, rest], mine_far),
            )
        )
    ]
    for copy in staged:
        copy.start()
    copy = functools.partial(remote, send=send, recv=recv)
    lend_far = copy(partial.at[2 - 2 * out, first], from_near, n=0, offset=-out)
    lend_near = copy(partial.at[2 + out, rest], from_far, n=1, offset=-out)
    to_side = copy(partial.at[2 - out], side, n=2, offset=-out)
    to_far = copy(partial.at[2 + 2 * out], behind, n=3, offset=2 * out)
    sum_near = copy(mine_near, ahead.at[first], n=4, offset=out)
    sum_far = copy(mine_far, ahead.at[rest], n=5, offset=-2 * out)
    entry_barrier()

    @pl.when(in_ok)
    def _():
        lend_far.start()

    @pl.when(out_ok)
    def _():
        lend_near.start()
        to_far.start()

    to_side.start()
    for c in staged:
        c.wait()

    def add(mine, theirs):
        mine[...] = (mine[...].astype(f32) + theirs[...].astype(f32)).astype(bf16)

    @pl.when(out_ok)
    def _():
        lend_far.wait_recv()
        add(mine_near, from_near)
        sum_near.start()

    @pl.when(in_ok)
    def _():
        lend_near.wait_recv()
        add(mine_far, from_far)
        sum_far.start()

    to_side.wait()

    @pl.when(out_ok)
    def _():
        lend_near.wait_send()
        to_far.wait_send()
        sum_near.wait()
        sum_far.wait_recv()

    @pl.when(in_ok)
    def _():
        lend_far.wait_send()
        to_far.wait_recv()
        sum_far.wait_send()


def sum_kernel(partial, side, behind, ahead, leaf, parent, got, leaf_sum, parent_sum, get, put):
    pieces = (pl.ds(6, 1), pl.ds(0, 2), pl.ds(2, 2), pl.ds(4, 2))
    gets = [
        [
            pltpu.make_async_copy(src.at[rows], got.at[n, rows], get.at[4 * p + n])
            for n, src in enumerate((partial.at[2], side, behind, ahead))
        ]
        for p, rows in enumerate(pieces)
    ]
    for piece in gets:
        for copy in piece:
            copy.start()
    _, out_ok, in_ok = sides()

    def total(r):
        s = got[0, r].astype(f32) + got[1, r].astype(f32)
        s = s + jnp.where(in_ok, got[2, r].astype(f32), 0.0)
        return s + jnp.where(out_ok, got[3, r].astype(f32), 0.0)

    for copy in gets[0]:
        copy.wait()
    tails = total(6)
    puts = []
    for c in range(3):
        for copy in gets[1 + c]:
            copy.wait()
        for q in range(2):
            s = total(2 * c + q)
            leaf_sum[c, 128 * q : 128 * q + 128, :] = s[0:128]
            parent_sum[c, :, 128 * q : 128 * q + 128] = s[128:144]
        leaf_sum[c, 256:296, :] = tails[40 * c : 40 * c + 40]
        shifted = tails[128:144] if c == 0 else pltpu.roll(tails[128:144], 128 - 40 * c, 1)
        parent_sum[c, :, 256:296] = shifted[:, :40]
        puts.append(pltpu.make_async_copy(leaf_sum.at[c], leaf.at[c], put.at[c]))
        puts[c].start()
    puts.append(pltpu.make_async_copy(parent_sum, parent, put.at[3]))
    puts[3].start()
    for copy in puts:
        copy.wait()


def on_device(multipole, m2m_ops, m2l_ops, lt, ls, pt, ps):
    mp = jnp.transpose(multipole, (1, 2, 0))
    pt, ps = jnp.transpose(pt[0]), jnp.transpose(ps[0])
    hbm = pl.BlockSpec(memory_space=pltpu.HBM)
    semaphores = pltpu.SemaphoreType.DMA
    rem, par, idx = pl.pallas_call(
        exchange_kernel,
        out_shape=(
            jax.ShapeDtypeStruct((SPAN, 3, P_SIZE, BOX_DEV), bf16),
            jax.ShapeDtypeStruct((SPAN, 7, PAR_DEV, 128), bf16),
            jax.ShapeDtypeStruct((2, 72, 128), jnp.int32),
        ),
        in_specs=[hbm] * 6,
        out_specs=(hbm, hbm, hbm),
        scratch_shapes=[
            pltpu.VMEM((3, P_SIZE, BOX_DEV), bf16),
            pltpu.VMEM((8, P_SIZE, P_SIZE), bf16),
            pltpu.VMEM((7, PAR_DEV, 128), bf16),
            pltpu.VMEM((CLASSES, SLOT), jnp.int32),
            pltpu.VMEM((CLASSES, SLOT), jnp.int32),
            pltpu.VMEM((PSLOT, CLASSES), jnp.int32),
            pltpu.VMEM((PSLOT, CLASSES), jnp.int32),
            pltpu.VMEM((CLASSES * 8 + 8, 128), f32),
            pltpu.VMEM((CLASSES, 128), f32),
            pltpu.VMEM((CLASSES * 8 + 8, 128), f32),
            pltpu.VMEM((2, 72, 128), jnp.int32),
            semaphores((6,)),
            semaphores((6,)),
            semaphores((4,)),
            semaphores((4,)),
            semaphores((8,)),
        ],
        compiler_params=pltpu.CompilerParams(
            collective_id=0, has_side_effects=True, vmem_limit_bytes=VMEM_BYTES
        ),
        name="exchange",
    )(mp, m2m_ops, lt[0], ls[0], pt, ps)
    partial = pl.pallas_call(
        translate_kernel,
        out_shape=jax.ShapeDtypeStruct((SPAN, 7, BOX_DEV + PAR_DEV, 128), bf16),
        in_specs=[hbm] * 5,
        out_specs=hbm,
        scratch_shapes=[
            pltpu.SMEM((2, 72, 128), jnp.int32),
            pltpu.VMEM((SPAN, 3, P_SIZE, BOX_DEV), bf16),
            pltpu.VMEM((SPAN, 7, PAR_DEV, 128), bf16),
            pltpu.VMEM((SPAN, 7, BOX_DEV + PAR_DEV, 128), bf16),
            pltpu.VMEM((ROWS * 8 + 8, 128), f32),
        ]
        + [pltpu.VMEM((SLOTS * 8 + 8, 128), f32)] * 4
        + [pltpu.VMEM((CLASSES, P_SIZE, P_SIZE), bf16), semaphores((CLASSES,)), semaphores((12,))]
        + [pltpu.VMEM((ACC_ROWS * 8, 128), f32)] * CHAINS,
        compiler_params=pltpu.CompilerParams(vmem_limit_bytes=VMEM_BYTES),
        name="translate",
    )(idx, mp, rem, par, m2l_ops)
    block = (7, BOX_DEV + PAR_DEV, 128)
    results = (
        jax.ShapeDtypeStruct((3, P_SIZE, BOX_DEV), f32),
        jax.ShapeDtypeStruct((3, PAR_DEV, P_SIZE), f32),
    )
    side, behind, ahead = pl.pallas_call(
        return_kernel,
        out_shape=(jax.ShapeDtypeStruct(block, bf16),) * 3,
        in_specs=[hbm],
        out_specs=(hbm,) * 3,
        scratch_shapes=[
            pltpu.VMEM((4,) + block[1:], bf16),
            pltpu.VMEM((3,) + block[1:], bf16),
            pltpu.VMEM((4,) + block[1:], bf16),
            pltpu.VMEM((3,) + block[1:], bf16),
            semaphores((6,)),
            semaphores((6,)),
            semaphores((2,)),
        ],
        compiler_params=pltpu.CompilerParams(
            collective_id=1, has_side_effects=True, vmem_limit_bytes=VMEM_BYTES
        ),
        name="return",
    )(partial)
    leaf, parent = pl.pallas_call(
        sum_kernel,
        out_shape=results,
        in_specs=[hbm] * 4,
        out_specs=(hbm, hbm),
        scratch_shapes=[
            pltpu.VMEM((4,) + block, bf16),
            pltpu.VMEM((3, P_SIZE, BOX_DEV), f32),
            pltpu.VMEM((3, PAR_DEV, P_SIZE), f32),
            semaphores((16,)),
            semaphores((4,)),
        ],
        compiler_params=pltpu.CompilerParams(vmem_limit_bytes=VMEM_BYTES),
        name="sums",
    )(partial, side, behind, ahead)
    return jnp.transpose(leaf, (2, 0, 1)), jnp.transpose(parent, (1, 0, 2))


def solution(mesh):
    boxes = P(("gx", "gy"), None, None)
    return jax.shard_map(
        on_device,
        mesh=mesh,
        in_specs=(boxes, P(), P(), boxes, boxes, boxes, boxes),
        out_specs=(boxes, boxes),
        check_vma=False,
    )
```
